512 devices in a mesh: ab: 32 (over x_lo, y, core), cd: 16 (over x_hi, z).
Axes of the slice: x: 4 (x_hi: 2, x_lo: 2; x = x_hi * 2 + x_lo), y: 8, z: 8, core: 2. Of those that a mesh axis runs over, the one named last changes fastest.
Arguments:
- integrals: bfloat16 [12800, 83200], P('ab', 'cd'), may hold values from -0.0390625 to 0.0390625
- doubles: bfloat16 [2048, 83200], P('ab', 'cd'), may hold values from -6 to 6
- singles: float32 [160, 400], replicated, may hold values from -6 to 6
Outputs:
- ladder: float32 [8, 12800, 64], P(None, ('ab', 'cd'))
The draws below stay inside these ranges and needn't reach their ends.
All inputs are finite; a program needn't handle non-finite values.
Results may differ from the reference program's by a relative error of at most 0.0029.
Values may be sent and summed in bfloat16 or wider, within the bound.
A program may use at most 64 MiB of HBM per device.

```python
import jax
import jax.numpy as jnp
from jax import lax

O = 160
V = 400
C_WIN = 208
ROW_BLK = 400
PAIR_DEV = 64
STEPS = 8
AB_ROWS = 12800
PAIRS = 2048
CD = 83200
N_AB = 32


def spiked(drawn, own_key, source, target, parts, factor):
    owner, partner = [(jnp.arange(drawn.shape[axis_at]) // (drawn.shape[axis_at] // parts)).reshape([-1 if axis == axis_at else 1 for axis in range(drawn.ndim)]) for axis_at in (source, target)]
    chosen = jax.random.permutation(own_key, parts)[partner]
    strong = (owner == chosen) | (owner == (partner + parts // 2) % parts)
    return jnp.where(strong, factor * drawn, drawn)


def block_levels(rng, dims, split, smallest, high):
    def one(axis_at, shards_of):
        heights = jax.random.uniform(jax.random.fold_in(jax.random.fold_in(rng, 6), axis_at), (shards_of,), jnp.float32, smallest / len(split), high / len(split))
        return jnp.repeat(jnp.exp(heights), dims[axis_at] // shards_of).reshape((-1,) + (1,) * (len(dims) - axis_at - 1))

    loudness = one(*split[0])
    for cut in split[1:]:
        loudness = loudness * one(*cut)
    return loudness


def gaussian(own_key, shape, scale, bound, split=(), kind=jnp.bfloat16):
    values = jax.random.normal(own_key, shape, jnp.float32) * scale
    if len(split) > 0:
        values = block_levels(own_key, shape, split, -0.22, 0.18) * values
    return jnp.clip(values, min=-bound, max=bound).astype(kind)


def bell_draw_with(stream_key, dims, deviation, bound, cuts, heavy, held_as=jnp.bfloat16):
    entries = deviation * jax.random.normal(stream_key, dims, jnp.float32)
    if cuts:
        entries = entries * block_levels(stream_key, dims, cuts, -0.22, 0.18)
    return jnp.clip(spiked(entries, jax.random.fold_in(stream_key, 3), *heavy), -bound, bound).astype(held_as)


def setup_inputs(seed: int = 0) -> dict:
    arg_keys = jax.random.split(jax.random.key(seed), 4)
    return {
        "integrals": bell_draw_with(arg_keys[0], (AB_ROWS, CD), CD ** -0.5, 0.0390625, ((0, 32), (1, 16)), (1, 0, 32, 2.75)),
        "doubles": gaussian(arg_keys[1], (PAIRS, CD), 1.0, 6.0, ((0, 32), (1, 16))),
        "singles": gaussian(arg_keys[2], (O, V), 1.0, 6.0, (), jnp.float32),
    }


def form_tau(pieces):
    double_rows, left_rows, right_rows = pieces
    amplitude = double_rows.astype(jnp.float32).reshape(PAIR_DEV, C_WIN, V) + left_rows[:, :, None] * right_rows[:, None, :]
    return amplitude.reshape(PAIR_DEV, CD).astype(jnp.bfloat16)


def reference(integrals, doubles, singles):
    pair_ids = jnp.arange(PAIRS, dtype=jnp.int32)
    left_rows = jnp.take(singles, pair_ids // O, axis=0)[:, :C_WIN]
    right_rows = jnp.take(singles, pair_ids % O, axis=0)
    tau_blocks = lax.map(form_tau, (doubles.reshape(N_AB, PAIR_DEV, CD), left_rows.reshape(N_AB, PAIR_DEV, C_WIN), right_rows.reshape(N_AB, PAIR_DEV, V)))
    offsets = jnp.arange(STEPS, dtype=jnp.int32) - (STEPS // 2 - 1)

    def block_rows(block_index):
        strip = lax.dynamic_slice_in_dim(integrals, (block_index * ROW_BLK).astype(jnp.int32), ROW_BLK, 0)
        chosen = jnp.take(tau_blocks, ((block_index - offsets) % N_AB).astype(jnp.int32), axis=0).reshape(STEPS * PAIR_DEV, CD)
        product = jnp.dot(strip, chosen.T, preferred_element_type=jnp.float32)
        return product.reshape(ROW_BLK, STEPS, PAIR_DEV)

    result = lax.map(block_rows, jnp.arange(N_AB, dtype=jnp.int32))
    return result.reshape(AB_ROWS, STEPS, PAIR_DEV).transpose(1, 0, 2)
```

```python
import functools

import jax
import jax.numpy as jnp
from jax import lax
from jax.experimental import pallas as pl
from jax.experimental.pallas import tpu as pltpu
from jax.sharding import PartitionSpec as P

MESH = pl.DeviceIdType.MESH
F32 = jnp.float32
BF16 = jnp.bfloat16
N_Z = 8
KC = 1024


def kernel(
    a_hbm, d_hbm, s_hbm, o_ref,
    a_v, s_v, slots, rtab, ltab, acc, acc_h,
    sbuf, rbuf, xsend, xrecv, tot, hsend, hrecv,
    loc_sem, up_s, up_r, dn_s, dn_r, fu_s, fu_r, fd_s, fd_r, sib_s, sib_r,
    z_s, z_r, x_s, x_r, h_s, h_r,
):
    pairs, cols = d_hbm.shape
    rows = a_hbm.shape[0]
    occ, virt = s_hbm.shape
    c_local = cols // virt
    n_ab = lax.axis_size("ab")
    n_cd = lax.axis_size("cd")
    n_x = n_cd // N_Z
    take = rows // n_cd
    half = pairs // 2

    ab = lax.axis_index("ab")
    cd = lax.axis_index("cd")
    core = lax.rem(ab, 2)
    chip2 = ab - core
    x_hi = cd // N_Z
    z = lax.rem(cd, N_Z)

    nxt = {"ab": lax.rem(ab + 2, n_ab)}
    prv = {"ab": lax.rem(ab + n_ab - 2, n_ab)}
    sib = {"ab": ab + 1 - 2 * core}
    low = {"ab": lax.rem(ab + n_ab - 1, n_ab)}
    high = {"ab": lax.rem(ab + 1, n_ab)}

    def member(k):
        return {"cd": lax.rem(cd + k, n_cd)}

    bar = pltpu.get_barrier_semaphore()
    for peer in (nxt, prv, low, high):
        pl.semaphore_signal(bar, inc=1, device_id=peer, device_id_type=MESH)

    def greet(k, carry):
        pl.semaphore_signal(bar, inc=1, device_id=member(k), device_id_type=MESH)
        return carry

    lax.fori_loop(1, n_cd, greet, 0)

    load_s = pltpu.make_async_copy(s_hbm, s_v, loc_sem.at[0])
    load_d = pltpu.make_async_copy(d_hbm, slots.at[0, core], loc_sem.at[1])
    load_a = pltpu.make_async_copy(a_hbm, a_v, loc_sem.at[2])
    load_s.start()
    load_d.start()
    load_a.start()

    pl.semaphore_wait(bar, n_cd + 3)

    def remote(src, dst, ss, rs, dev):
        return pltpu.make_async_remote_copy(
            src_ref=src, dst_ref=dst, send_sem=ss, recv_sem=rs, device_id=dev, device_id_type=MESH
        )

    part = [pl.ds(i * half, half) for i in range(2)]
    up = [remote(d_hbm.at[q], slots.at[1, core, q], up_s.at[i], up_r.at[i], nxt) for i, q in enumerate(part)]
    dn = [remote(d_hbm.at[q], slots.at[2, core, q], dn_s.at[i], dn_r.at[i], prv) for i, q in enumerate(part)]
    fu = [remote(slots.at[1, core, q], slots.at[3, core, q], fu_s.at[i], fu_r.at[i], nxt) for i, q in enumerate(part)]
    fd = [remote(slots.at[2, core, q], slots.at[3, core, q], fd_s.at[i], fd_r.at[i], low) for i, q in enumerate(part)]
    own = remote(d_hbm, slots.at[0, core], sib_s.at[6], sib_r.at[6], sib)
    sh_up = [remote(slots.at[1, core, q], slots.at[1, core, q], sib_s.at[i], sib_r.at[i], sib) for i, q in enumerate(part)]
    sh_dn = [remote(slots.at[2, core, q], slots.at[2, core, q], sib_s.at[2 + i], sib_r.at[2 + i], sib) for i, q in enumerate(part)]
    sh_fu = [remote(slots.at[3, 1, q], slots.at[3, 1, q], sib_s.at[4 + i], sib_r.at[4 + i], sib) for i, q in enumerate(part)]

    for i in range(2):
        up[i].start()
        dn[i].start()
    own.start()

    load_s.wait()

    def spread(t, carry):
        rows_t = s_v[pl.ds(pl.multiple_of(lax.rem(32 * t, occ), 32), 32), :]
        at = pl.ds(pl.multiple_of(32 * t, 32), 32)
        for c in range(c_local):
            rtab[at, c * virt : (c + 1) * virt] = rows_t
        return carry

    lax.fori_loop(0, rtab.shape[0] // 32, spread, 0)
    few = s_v[0 : ltab.shape[0], :]
    lane = lax.broadcasted_iota(jnp.int32, few.shape, 1)
    for c in range(c_local):
        value = jnp.sum(jnp.where(lane == cd * c_local + c, few, 0.0), axis=1, keepdims=True)
        for i in range(few.shape[0]):
            ltab[i, :, c * virt : (c + 1) * virt] = jnp.broadcast_to(value[i : i + 1, :], (8, virt))

    def block(offset):
        g = lax.rem(chip2 + offset + n_ab, n_ab)
        first = g * pairs
        i0 = first // occ
        return i0, occ * (i0 + 1) - first, pl.multiple_of(lax.rem(first, occ), 32)

    def tau(slot, h, who, r0, count, ks, width):
        i0, turn, j0 = who
        raw = slots[slot, h, pl.ds(r0, count), ks].astype(F32)
        right = rtab[pl.ds(pl.multiple_of(j0 + r0, 32), count), ks]
        pair = lax.broadcasted_iota(jnp.int32, (count, width), 0) + r0
        before, after = (jnp.concatenate([ltab[i, :, ks]] * (count // 8), axis=0) for i in (i0, i0 + 1))
        left = jnp.where(pair < turn, before, after)
        return (raw + left * right).astype(BF16)

    def product(slot, whos, r0, count, out):
        def piece(ks, width):
            both = jnp.concatenate([tau(slot, h, whos[h], r0, count, ks, width) for h in range(2)], axis=0)
            return lax.dot_general(a_v[:, ks], both, (((1,), (1,)), ((), ())), preferred_element_type=F32)

        whole = cols // KC
        out[0:rows, :] = piece(pl.ds(whole * KC, cols - whole * KC), cols - whole * KC)

        def step(t, carry):
            out[0:rows, :] += piece(pl.ds(pl.multiple_of(t * KC, KC), KC), KC)
            return carry

        lax.fori_loop(0, whole, step, 0)

    def z_copy(s, k):
        to = lax.rem(z + k, N_Z)
        return remote(
            sbuf.at[s, to], rbuf.at[s, k - 1], z_s.at[s, k - 1], z_r.at[s, k - 1], {"cd": x_hi * N_Z + to}
        )

    def scatter(s):
        for j in range(n_cd):
            sbuf[s, j % N_Z, j // N_Z, :, :] = acc[j * take : j * take + 32, :].astype(sbuf.dtype)

        def send(k, carry):
            z_copy(s, k).start()
            return carry

        lax.fori_loop(1, N_Z, send, 0)

    def x_copy(s):
        return remote(xsend.at[s], xrecv.at[s], x_s.at[s], x_r.at[s], {"cd": (1 - x_hi) * N_Z + z})

    def gather(s):
        def arrive(k, carry):
            z_copy(s, k).wait_recv()
            return carry

        lax.fori_loop(1, N_Z, arrive, 0)
        for dst, xo in ((xsend, 1 - x_hi), (tot, x_hi)):
            total = sbuf[s, z, xo].astype(F32)
            for k in range(N_Z - 1):
                total = total + rbuf[s, k, xo].astype(F32)
            dst[s] = total
        x_copy(s).start()

    first_k = [3 + core, 2 + core, 5 + core, 4 + core, 1 + core, core, 7 - 7 * core, 6 + core]

    def finish(s):
        x_copy(s).wait_recv()
        value = tot[s] + xrecv[s]
        for h in range(2):
            o_ref[first_k[2 * s + h], :, :] = value[0:take, h * pairs : (h + 1) * pairs]

    top = (take + 1) // 2

    def h_copy(i, k):
        to = lax.rem(cd + k, n_cd)
        return remote(hsend.at[i, to], hrecv.at[i, k - 1], h_s.at[i, k - 1], h_r.at[i, k - 1], {"cd": to})

    def scatter_half(i):
        for j in range(n_cd):
            a = acc_h[j * take : j * take + 16, :]
            b = acc_h[j * take + top : j * take + top + 16, :]
            hsend[i, j, :, :] = jnp.concatenate([a, b], axis=1).astype(hsend.dtype)

        def send(k, carry):
            h_copy(i, k).start()
            return carry

        lax.fori_loop(1, n_cd, send, 0)

    def finish_half(i):
        def arrive(k, carry):
            h_copy(i, k).wait_recv()
            return carry

        lax.fori_loop(1, n_cd, arrive, 0)
        value = hsend[i, cd].astype(F32)
        for k in range(n_cd - 1):
            value = value + hrecv[i, k].astype(F32)
        for h in range(2):
            k = first_k[6 + h]
            o_ref[k, 0:top, i * half : (i + 1) * half] = value[0:top, h * half : (h + 1) * half]
            o_ref[k, top:take, i * half : (i + 1) * half] = value[
                0 : take - top, pairs + h * half : pairs + (h + 1) * half
            ]

    acc[rows:, :] = jnp.zeros((acc.shape[0] - rows, acc.shape[1]), F32)
    acc_h[rows:, :] = jnp.zeros((acc_h.shape[0] - rows, acc_h.shape[1]), F32)

    load_d.wait()
    load_a.wait()
    own.wait_recv()
    product(0, (block(0), block(1)), 0, pairs, acc)
    scatter(0)

    for i in range(2):
        up[i].wait_recv()
        fu[i].start()
        sh_up[i].start()
        dn[i].wait_recv()

        @pl.when(core == 0)
        def _():
            fd[i].start()

        sh_dn[i].start()
        if i == 0:
            gather(0)
    for i in range(2):
        sh_up[i].wait_recv()
    product(1, (block(-2), block(-1)), 0, pairs, acc)
    scatter(1)
    for i in range(2):
        sh_dn[i].wait_recv()
    product(2, (block(2), block(3)), 0, pairs, acc)
    scatter(2)
    finish(0)

    last = (block(jnp.where(core == 0, -4, 4)), block(-3))
    for i in range(2):
        fu[i].wait_recv()

        @pl.when(core == 1)
        def _():
            sh_fu[i].start()
            fd[i].wait_recv()

        if i == 0:
            gather(1)
            gather(2)

        @pl.when(core == 0)
        def _():
            sh_fu[i].wait_recv()

        product(3, last, i * half, half, acc_h)
        scatter_half(i)
        if i == 0:
            finish(1)
            finish(2)
    finish_half(0)
    finish_half(1)

    for i in range(2):
        up[i].wait_send()
        dn[i].wait_send()
        fu[i].wait_send()
        sh_up[i].wait_send()
        sh_dn[i].wait_send()

        @pl.when(core == 0)
        def _():
            fd[i].wait_send()

        @pl.when(core == 1)
        def _():
            sh_fu[i].wait_send()

    own.wait_send()
    for s in range(3):
        x_copy(s).wait_send()

        def sent(k, carry, s=s):
            z_copy(s, k).wait_send()
            return carry

        lax.fori_loop(1, N_Z, sent, 0)
    for i in range(2):

        def sent_half(k, carry, i=i):
            h_copy(i, k).wait_send()
            return carry

        lax.fori_loop(1, n_cd, sent_half, 0)


def shards(integrals, doubles, singles):
    rows, cols = integrals.shape
    pairs = doubles.shape[0]
    occ, virt = singles.shape
    n_ab, n_cd = lax.axis_size("ab"), lax.axis_size("cd")
    steps = n_ab // 4
    take = rows // n_cd
    dma = pltpu.SemaphoreType.DMA
    return pl.pallas_call(
        kernel,
        out_shape=jax.ShapeDtypeStruct((steps, take, pairs), F32),
        in_specs=[pl.BlockSpec(memory_space=pl.ANY)] * 3,
        out_specs=pl.BlockSpec(memory_space=pltpu.VMEM),
        scratch_shapes=[
            pltpu.VMEM((rows, cols), BF16),
            pltpu.VMEM((occ, virt), F32),
            pltpu.VMEM((4, 2, pairs, cols), BF16),
            pltpu.VMEM((occ + 32, cols), F32),
            pltpu.VMEM((16, 8, cols), F32),
            pltpu.VMEM((rows + 8, 2 * pairs), F32),
            pltpu.VMEM((rows + 8, pairs), F32),
            pltpu.VMEM((3, N_Z, n_cd // N_Z, 32, 2 * pairs), F32),
            pltpu.VMEM((3, N_Z - 1, n_cd // N_Z, 32, 2 * pairs), F32),
            pltpu.VMEM((3, 32, 2 * pairs), F32),
            pltpu.VMEM((3, 32, 2 * pairs), F32),
            pltpu.VMEM((3, 32, 2 * pairs), F32),
            pltpu.VMEM((2, n_cd, 16, 2 * pairs), BF16),
            pltpu.VMEM((2, n_cd - 1, 16, 2 * pairs), BF16),
            dma((3,)),
            dma((2,)), dma((2,)), dma((2,)), dma((2,)),
            dma((2,)), dma((2,)), dma((2,)), dma((2,)),
            dma((7,)), dma((7,)),
            dma((3, N_Z - 1)), dma((3, N_Z - 1)),
            dma((3,)), dma((3,)),
            dma((2, n_cd - 1)), dma((2, n_cd - 1)),
        ],
        compiler_params=pltpu.CompilerParams(
            collective_id=0, has_side_effects=True, vmem_limit_bytes=48 * 2**20
        ),
        cost_estimate=pl.CostEstimate(
            flops=2 * rows * cols * steps * pairs, bytes_accessed=2 * (rows + pairs) * cols, transcendentals=0
        ),
    )(integrals, doubles, singles)


def solution(mesh):
    in_specs = (P("ab", "cd"), P("ab", "cd"), P())
    out_specs = P(None, ("ab", "cd"), None)
    return jax.shard_map(shards, mesh=mesh, in_specs=in_specs, out_specs=out_specs, check_vma=False)
```

```python
import functools

import jax
import jax.numpy as jnp
from jax import lax
from jax.experimental import pallas as pl
from jax.experimental.pallas import tpu as pltpu
from jax.sharding import PartitionSpec as P

MESH = pl.DeviceIdType.MESH
F32 = jnp.float32
BF16 = jnp.bfloat16
N_Z = 8
KC = 1024


def kernel(
    a_hbm, d_hbm, s_hbm, o_ref,
    a_v, s_v, slots, rtab, ltab, acc, acc_l,
    sbuf, rbuf, xsend, xrecv, tot, hsend, hrecv, lsend, lrecv,
    loc_sem, up_s, up_r, dn_s, dn_r, fd_s, fd_r, f1_s, f1_r, f0_s, f0_r, sib_s, sib_r,
    z_s, z_r, x_s, x_r, h_s, h_r, l_s, l_r,
):
    pairs, cols = d_hbm.shape
    rows = a_hbm.shape[0]
    occ, virt = s_hbm.shape
    c_local = cols // virt
    n_ab = lax.axis_size("ab")
    n_cd = lax.axis_size("cd")
    n_x = n_cd // N_Z
    take = rows // n_cd
    half = pairs // 2

    ab = lax.axis_index("ab")
    cd = lax.axis_index("cd")
    core = lax.rem(ab, 2)
    chip2 = ab - core
    x_hi = cd // N_Z
    z = lax.rem(cd, N_Z)

    nxt = {"ab": lax.rem(ab + 2, n_ab)}
    prv = {"ab": lax.rem(ab + n_ab - 2, n_ab)}
    sib = {"ab": ab + 1 - 2 * core}
    low = {"ab": lax.rem(ab + n_ab - 1, n_ab)}
    high = {"ab": lax.rem(ab + 1, n_ab)}
    nxt0 = {"ab": lax.rem(chip2 + 2, n_ab)}

    bar = pltpu.get_barrier_semaphore()
    for peer in (nxt, prv, low, high):
        pl.semaphore_signal(bar, inc=1, device_id=peer, device_id_type=MESH)

    def greet(k, carry):
        pl.semaphore_signal(bar, inc=1, device_id={"cd": lax.rem(cd + k, n_cd)}, device_id_type=MESH)
        return carry

    lax.fori_loop(1, n_cd, greet, 0)

    load_s = pltpu.make_async_copy(s_hbm, s_v, loc_sem.at[0])
    load_d = pltpu.make_async_copy(d_hbm, slots.at[0, core], loc_sem.at[1])
    load_a = pltpu.make_async_copy(a_hbm, a_v, loc_sem.at[2])
    load_s.start()
    load_d.start()
    load_a.start()

    pl.semaphore_wait(bar, n_cd + 3)

    def remote(src, dst, ss, rs, dev):
        return pltpu.make_async_remote_copy(
            src_ref=src, dst_ref=dst, send_sem=ss, recv_sem=rs, device_id=dev, device_id_type=MESH
        )

    part = [pl.ds(pl.multiple_of(half * r, 32), half) for r in (core, 1 - core)]
    other = [pl.ds(pl.multiple_of(half * r, 32), half) for r in (1 - core, core)]
    up = [remote(d_hbm.at[q], slots.at[1, core, q], up_s.at[i], up_r.at[i], nxt) for i, q in enumerate(part)]
    dn = [remote(d_hbm.at[q], slots.at[2, core, q], dn_s.at[i], dn_r.at[i], prv) for i, q in enumerate(part)]
    own = remote(d_hbm, slots.at[0, core], sib_s.at[5], sib_r.at[5], sib)
    sh_up = [remote(slots.at[1, core, q], slots.at[1, core, q], sib_s.at[i], sib_r.at[i], sib) for i, q in enumerate(part)]
    sh_dn = [remote(slots.at[2, core, q], slots.at[2, core, q], sib_s.at[2 + i], sib_r.at[2 + i], sib) for i, q in enumerate(part)]
    f1 = remote(slots.at[1, 1, part[1]], slots.at[3, 1, part[1]], f1_s, f1_r, nxt)
    sh_f1 = remote(slots.at[3, 1, part[1]], slots.at[3, 1, part[1]], sib_s.at[4], sib_r.at[4], sib)
    f0 = remote(slots.at[1, 0, part[0]], slots.at[3, 0, part[0]], f0_s, f0_r.at[core], nxt0)
    f0_in = [
        remote(slots.at[1, 0, pl.ds(i * half, half)], slots.at[3, 0, pl.ds(i * half, half)], f0_s, f0_r.at[i], nxt0)
        for i in range(2)
    ]
    fd = [remote(slots.at[2, core, q], slots.at[3, core, q], fd_s.at[i], fd_r.at[i], low) for i, q in enumerate(part)]
    fd_in = [remote(slots.at[2, 0, q], slots.at[3, 0, q], fd_s.at[i], fd_r.at[i], low) for i, q in enumerate(other)]

    for i in range(2):
        up[i].start()
        dn[i].start()
        if i == 0:
            own.start()

    load_s.wait()

    def spread(t, carry):
        rows_t = s_v[pl.ds(pl.multiple_of(lax.rem(32 * t, occ), 32), 32), :]
        at = pl.ds(pl.multiple_of(32 * t, 32), 32)
        for c in range(c_local):
            rtab[at, c * virt : (c + 1) * virt] = rows_t
        return carry

    lax.fori_loop(0, rtab.shape[0] // 32, spread, 0)
    few = s_v[0 : ltab.shape[0], :]
    lane = lax.broadcasted_iota(jnp.int32, few.shape, 1)
    for c in range(c_local):
        value = jnp.sum(jnp.where(lane == cd * c_local + c, few, 0.0), axis=1, keepdims=True)
        for i in range(few.shape[0]):
            ltab[i, :, c * virt : (c + 1) * virt] = jnp.broadcast_to(value[i : i + 1, :], (8, virt))

    far = jnp.where(core == 0, -4, 4)
    place = {(0, 0): 0, (0, 1): 1, (1, 0): -2, (1, 1): -1, (2, 0): 2, (2, 1): 3, (3, 0): far, (3, 1): -3}
    first_k = {
        (0, 0): 3 + core, (0, 1): 2 + core, (1, 0): 5 + core, (1, 1): 4 + core,
        (2, 0): 1 + core, (2, 1): core, (3, 0): 7 - 7 * core, (3, 1): 6 + core,
    }

    def tau(slot, h, r0, count, ks, width):
        first = lax.rem(chip2 + place[slot, h] + n_ab, n_ab) * pairs
        i0 = first // occ
        turn = occ * (i0 + 1) - first
        raw = slots[slot, h, r0 : r0 + count, ks].astype(F32)
        right = rtab[pl.ds(pl.multiple_of(lax.rem(first, occ) + r0, 32), count), ks]
        pair = lax.broadcasted_iota(jnp.int32, (count, width), 0) + r0
        before, after = (jnp.concatenate([ltab[i, :, ks]] * (count // 8), axis=0) for i in (i0, i0 + 1))
        left = jnp.where(pair < turn, before, after)
        return (raw + left * right).astype(BF16)

    def product(parts, out):
        total = sum(p[3] for p in parts)

        def piece(ks, width):
            formed = [tau(*p, ks, width) for p in parts]
            both = jnp.concatenate(formed, axis=0) if len(formed) > 1 else formed[0]
            return lax.dot_general(a_v[:, ks], both, (((1,), (1,)), ((), ())), preferred_element_type=F32)

        whole = cols // KC
        out[0:rows, 0:total] = piece(pl.ds(whole * KC, cols - whole * KC), cols - whole * KC)

        def step(t, carry):
            out[0:rows, 0:total] += piece(pl.ds(pl.multiple_of(t * KC, KC), KC), KC)
            return carry

        lax.fori_loop(0, whole, step, 0)

    def put(value, parts):
        lane0 = 0
        for slot, h, r0, count in parts:
            o_ref[first_k[slot, h], :, r0 : r0 + count] = value[0:take, lane0 : lane0 + count]
            lane0 += count

    def z_copy(s, k):
        to = lax.rem(z + k, N_Z)
        return remote(
            sbuf.at[s, to], rbuf.at[s, k - 1], z_s.at[s, k - 1], z_r.at[s, k - 1], {"cd": x_hi * N_Z + to}
        )

    def scatter(s):
        for j in range(n_cd):
            sbuf[s, j % N_Z, j // N_Z, :, :] = acc[j * take : j * take + 32, :].astype(sbuf.dtype)

        def send(k, carry):
            z_copy(s, k).start()
            return carry

        lax.fori_loop(1, N_Z, send, 0)

    def x_copy(s):
        return remote(xsend.at[s], xrecv.at[s], x_s.at[s], x_r.at[s], {"cd": (1 - x_hi) * N_Z + z})

    def gather(s):
        def arrive(k, carry):
            z_copy(s, k).wait_recv()
            return carry

        lax.fori_loop(1, N_Z, arrive, 0)
        for dst, xo in ((xsend, 1 - x_hi), (tot, x_hi)):
            total = sbuf[s, z, xo].astype(F32)
            for k in range(N_Z - 1):
                total = total + rbuf[s, k, xo].astype(F32)
            dst[s] = total
        x_copy(s).start()

    def finish(s, parts):
        x_copy(s).wait_recv()
        put(tot[s] + xrecv[s], parts)

    order = [(x, k) for k in (4, 3, 5, 2, 6, 1, 7, 0) for x in (1, 0) if x or k]

    def all_copies(send, recv, ss, rs):
        copies = []
        for x, k in order:
            to = lax.rem(x_hi + x, n_x) * N_Z + lax.rem(z + k, N_Z)
            n = 2 * k + x - 1
            copies.append(remote(send.at[to], recv.at[n], ss.at[n], rs.at[n], {"cd": to}))
        return copies

    def all_sum(send, recv, copies):
        for copy in reversed(copies):
            copy.wait_recv()
        value = send[cd].astype(F32)
        for n in range(n_cd - 1):
            value = value + recv[n].astype(F32)
        return value

    acc[rows:, :] = jnp.zeros((acc.shape[0] - rows, acc.shape[1]), F32)
    acc_l[rows:, :] = jnp.zeros((acc_l.shape[0] - rows, acc_l.shape[1]), F32)

    parts = [
        [(0, 0, 0, pairs), (0, 1, 0, pairs)],
        [(1, 0, 0, half), (1, 1, half, half), (2, 0, 0, half), (2, 1, half, half)],
        [(1, 0, half, half), (1, 1, 0, half), (2, 0, half, half), (2, 1, 0, half)],
    ]
    late = [(3, 1, 0, pairs), (3, 0, 0, half)]
    late_1 = [(3, 1, 0, pairs), (3, 0, 0, pairs)]
    last = [(3, 0, half, half)]

    load_d.wait()
    load_a.wait()
    own.wait_recv()
    product(parts[0], acc)
    scatter(0)

    up[0].wait_recv()
    sh_up[0].start()
    dn[0].wait_recv()
    sh_dn[0].start()
    sh_up_in = [remote(slots.at[1, 1 - core, q], slots.at[1, 1 - core, q], sib_s.at[i], sib_r.at[i], sib) for i, q in enumerate(other)]
    sh_dn_in = [remote(slots.at[2, 1 - core, q], slots.at[2, 1 - core, q], sib_s.at[2 + i], sib_r.at[2 + i], sib) for i, q in enumerate(other)]
    sh_f1_in = remote(slots.at[3, 1, part[0]], slots.at[3, 1, part[0]], sib_s.at[4], sib_r.at[4], sib)

    @pl.when(core == 0)
    def _():
        fd[0].start()
        sh_up_in[0].wait_recv()
        f1.start()
        f0.start()

    @pl.when(core == 1)
    def _():
        sh_up_in[0].wait_recv()

    sh_dn_in[0].wait_recv()
    product(parts[1], acc)
    scatter(1)

    up[1].wait_recv()
    sh_up[1].start()

    @pl.when(core == 1)
    def _():
        f1.start()

    dn[1].wait_recv()
    sh_dn[1].start()

    @pl.when(core == 0)
    def _():
        fd[1].start()

    sh_up_in[1].wait_recv()

    @pl.when(core == 1)
    def _():
        f0.start()

    sh_dn_in[1].wait_recv()
    product(parts[2], acc)
    scatter(2)
    gather(0)
    gather(1)

    f1.wait_recv()
    sh_f1.start()
    gather(2)
    h_copies = all_copies(hsend, hrecv, h_s, h_r)
    l_copies = all_copies(lsend, lrecv, l_s, l_r)

    @pl.when(core == 0)
    def _():
        f0_in[0].wait_recv()
        sh_f1_in.wait_recv()
        product(late, acc)

    @pl.when(core == 1)
    def _():
        fd_in[0].wait_recv()
        fd_in[1].wait_recv()
        sh_f1_in.wait_recv()
        product(late_1, acc)

    for j in range(n_cd):
        hsend[j, :, :] = acc[j * take : j * take + 32, :].astype(hsend.dtype)
    for copy in h_copies:
        copy.start()
    finish(0, parts[0])
    finish(1, parts[1])

    @pl.when(core == 0)
    def _():
        f0_in[1].wait_recv()
        product(last, acc_l)
        for j in range(n_cd):
            lsend[j, :, :] = jnp.concatenate(
                [acc_l[j * take + 7 * a : j * take + 7 * a + 8, :] for a in range(4)], axis=1
            )
        for copy in l_copies:
            copy.start()

    finish(2, parts[2])
    value = all_sum(hsend, hrecv, h_copies)
    put(value, late)

    @pl.when(core == 1)
    def _():
        o_ref[first_k[3, 0], :, half:pairs] = value[0:take, pairs + half : 2 * pairs]

    @pl.when(core == 0)
    def _():
        final = all_sum(lsend, lrecv, l_copies)
        for a in range(4):
            count = min(7, take - 7 * a)
            o_ref[first_k[3, 0], 7 * a : 7 * a + count, half:pairs] = final[0:count, a * half : (a + 1) * half]

    for copy in (*up, *dn, own, *sh_up, *sh_dn, f1, sh_f1, f0, *h_copies):
        copy.wait_send()

    @pl.when(core == 0)
    def _():
        for copy in (*fd, *l_copies):
            copy.wait_send()

    for s in range(3):
        x_copy(s).wait_send()

        def sent(k, carry, s=s):
            z_copy(s, k).wait_send()
            return carry

        lax.fori_loop(1, N_Z, sent, 0)


def shards(integrals, doubles, singles):
    rows, cols = integrals.shape
    pairs = doubles.shape[0]
    occ, virt = singles.shape
    n_ab, n_cd = lax.axis_size("ab"), lax.axis_size("cd")
    steps = n_ab // 4
    take = rows // n_cd
    dma = pltpu.SemaphoreType.DMA
    return pl.pallas_call(
        kernel,
        out_shape=jax.ShapeDtypeStruct((steps, take, pairs), F32),
        in_specs=[pl.BlockSpec(memory_space=pl.ANY)] * 3,
        out_specs=pl.BlockSpec(memory_space=pltpu.VMEM),
        scratch_shapes=[
            pltpu.VMEM((rows, cols), BF16),
            pltpu.VMEM((occ, virt), F32),
            pltpu.VMEM((4, 2, pairs, cols), BF16),
            pltpu.VMEM((occ + 32, cols), F32),
            pltpu.VMEM((16, 8, cols), F32),
            pltpu.VMEM((rows + 8, 2 * pairs), F32),
            pltpu.VMEM((rows + 8, pairs // 2), F32),
            pltpu.VMEM((3, N_Z, n_cd // N_Z, 32, 2 * pairs), BF16),
            pltpu.VMEM((3, N_Z - 1, n_cd // N_Z, 32, 2 * pairs), BF16),
            pltpu.VMEM((3, 32, 2 * pairs), F32),
            pltpu.VMEM((3, 32, 2 * pairs), F32),
            pltpu.VMEM((3, 32, 2 * pairs), F32),
            pltpu.VMEM((n_cd, 32, 2 * pairs), BF16),
            pltpu.VMEM((n_cd - 1, 32, 2 * pairs), BF16),
            pltpu.VMEM((n_cd, 8, 2 * pairs), F32),
            pltpu.VMEM((n_cd - 1, 8, 2 * pairs), F32),
            dma((3,)),
            dma((2,)), dma((2,)), dma((2,)), dma((2,)), dma((2,)), dma((2,)),
            dma, dma, dma, dma((2,)),
            dma((6,)), dma((6,)),
            dma((3, N_Z - 1)), dma((3, N_Z - 1)),
            dma((3,)), dma((3,)),
            dma((n_cd - 1,)), dma((n_cd - 1,)),
            dma((n_cd - 1,)), dma((n_cd - 1,)),
        ],
        compiler_params=pltpu.CompilerParams(
            collective_id=0, has_side_effects=True, vmem_limit_bytes=60 * 2**20
        ),
        cost_estimate=pl.CostEstimate(
            flops=2 * rows * cols * steps * pairs, bytes_accessed=2 * (rows + pairs) * cols, transcendentals=0
        ),
    )(integrals, doubles, singles)


def solution(mesh):
    in_specs = (P("ab", "cd"), P("ab", "cd"), P())
    out_specs = P(None, ("ab", "cd"), None)
    return jax.shard_map(shards, mesh=mesh, in_specs=in_specs, out_specs=out_specs, check_vma=False)
```

```python
import functools

import jax
import jax.numpy as jnp
from jax import lax
from jax.experimental import pallas as pl
from jax.experimental.pallas import tpu as pltpu
from jax.sharding import PartitionSpec as P

MESH = pl.DeviceIdType.MESH
F32 = jnp.float32
BF16 = jnp.bfloat16
N_Z = 8
KC = 1024
CUT = 4096


def kernel(
    a_hbm, d_hbm, s_hbm, o_ref,
    a_v, s_v, slots, rtab, ltab, acc, acc_l,
    sbuf, rbuf, xsend, xrecv, tot, lsend, lrecv,
    loc_sem, up_s, up_r, dn_s, dn_r, fd_s, fd_r, f1_s, f1_r, f0_s, f0_r, sib_s, sib_r,
    z_s, z_r, x_s, x_r, l_s, l_r,
):
    pairs, cols = d_hbm.shape
    rows = a_hbm.shape[0]
    occ, virt = s_hbm.shape
    c_local = cols // virt
    n_ab = lax.axis_size("ab")
    n_cd = lax.axis_size("cd")
    n_x = n_cd // N_Z
    take = rows // n_cd
    half = pairs // 2

    ab = lax.axis_index("ab")
    cd = lax.axis_index("cd")
    core = lax.rem(ab, 2)
    chip2 = ab - core
    x_hi = cd // N_Z
    z = lax.rem(cd, N_Z)

    nxt = {"ab": lax.rem(ab + 2, n_ab)}
    prv = {"ab": lax.rem(ab + n_ab - 2, n_ab)}
    sib = {"ab": ab + 1 - 2 * core}
    low = {"ab": lax.rem(ab + n_ab - 1, n_ab)}
    high = {"ab": lax.rem(ab + 1, n_ab)}
    nxt0 = {"ab": lax.rem(chip2 + 2, n_ab)}

    bar = pltpu.get_barrier_semaphore()
    for peer in (nxt, prv, low, high):
        pl.semaphore_signal(bar, inc=1, device_id=peer, device_id_type=MESH)

    def greet(k, carry):
        pl.semaphore_signal(bar, inc=1, device_id={"cd": lax.rem(cd + k, n_cd)}, device_id_type=MESH)
        return carry

    lax.fori_loop(1, n_cd, greet, 0)

    load_s = pltpu.make_async_copy(s_hbm, s_v, loc_sem.at[0])
    load_d = pltpu.make_async_copy(d_hbm, slots.at[0, core], loc_sem.at[1])
    load_a = pltpu.make_async_copy(a_hbm, a_v, loc_sem.at[2])
    load_s.start()
    load_d.start()
    load_a.start()

    pl.semaphore_wait(bar, n_cd + 3)

    def remote(src, dst, ss, rs, dev):
        return pltpu.make_async_remote_copy(
            src_ref=src, dst_ref=dst, send_sem=ss, recv_sem=rs, device_id=dev, device_id_type=MESH
        )

    part = [pl.ds(pl.multiple_of(half * r, 32), half) for r in (core, 1 - core)]
    other = [pl.ds(pl.multiple_of(half * r, 32), half) for r in (1 - core, core)]
    quarter = half // 2
    halved = [pl.ds(pl.multiple_of(half * (1 - core) + quarter * j, 16), quarter) for j in range(2)]
    up_rows = [part[0], *halved]
    up = [remote(d_hbm.at[q], slots.at[1, core, q], up_s.at[i], up_r.at[i], nxt) for i, q in enumerate(up_rows)]
    dn = [remote(d_hbm.at[q], slots.at[2, core, q], dn_s.at[i], dn_r.at[i], prv) for i, q in enumerate(part)]
    own = remote(d_hbm, slots.at[0, core], sib_s.at[5], sib_r.at[5], sib)
    sh_up = [remote(slots.at[1, core, q], slots.at[1, core, q], sib_s.at[i], sib_r.at[i], sib) for i, q in enumerate(part)]
    sh_dn = [remote(slots.at[2, core, q], slots.at[2, core, q], sib_s.at[2 + i], sib_r.at[2 + i], sib) for i, q in enumerate(part)]
    f1 = [remote(slots.at[1, 1, q], slots.at[3, 1, q], f1_s.at[j], f1_r.at[j], nxt) for j, q in enumerate(halved)]
    sh_f1 = remote(slots.at[3, 1, part[1]], slots.at[3, 1, part[1]], sib_s.at[4], sib_r.at[4], sib)
    spans = [pl.ds(0, CUT), pl.ds(CUT, cols - CUT)]
    f0 = [
        remote(slots.at[1, 0, part[0], c], slots.at[3, 0, part[0], c], f0_s.at[j], f0_r.at[core, j], nxt0)
        for j, c in enumerate(spans)
    ]
    f0_in = [
        [
            remote(slots.at[1, 0, q, c], slots.at[3, 0, q, c], f0_s.at[j], f0_r.at[i, j], nxt0)
            for i, q in enumerate((pl.ds(0, half), pl.ds(half, half)))
        ]
        for j, c in enumerate(spans)
    ]
    fd = [remote(slots.at[2, core, q], slots.at[3, core, q], fd_s.at[i], fd_r.at[i], low) for i, q in enumerate(part)]
    fd_in = [remote(slots.at[2, 0, q], slots.at[3, 0, q], fd_s.at[i], fd_r.at[i], low) for i, q in enumerate(other)]

    up[0].start()
    dn[0].start()
    own.start()
    up[1].start()
    up[2].start()
    dn[1].start()

    load_s.wait()

    def spread(t, carry):
        rows_t = s_v[pl.ds(pl.multiple_of(lax.rem(32 * t, occ), 32), 32), :]
        at = pl.ds(pl.multiple_of(32 * t, 32), 32)
        for c in range(c_local):
            rtab[at, c * virt : (c + 1) * virt] = rows_t
        return carry

    lax.fori_loop(0, rtab.shape[0] // 32, spread, 0)
    few = s_v[0 : ltab.shape[0], :]
    lane = lax.broadcasted_iota(jnp.int32, few.shape, 1)
    for c in range(c_local):
        value = jnp.sum(jnp.where(lane == cd * c_local + c, few, 0.0), axis=1, keepdims=True)
        for i in range(few.shape[0]):
            ltab[i, :, c * virt : (c + 1) * virt] = jnp.broadcast_to(value[i : i + 1, :], (8, virt))

    far = jnp.where(core == 0, -4, 4)
    place = {(0, 0): 0, (0, 1): 1, (1, 0): -2, (1, 1): -1, (2, 0): 2, (2, 1): 3, (3, 0): far, (3, 1): -3}
    first_k = {
        (0, 0): 3 + core, (0, 1): 2 + core, (1, 0): 5 + core, (1, 1): 4 + core,
        (2, 0): 1 + core, (2, 1): core, (3, 0): 7 - 7 * core, (3, 1): 6 + core,
    }

    def tau(slot, h, r0, count, ks, width):
        first = lax.rem(chip2 + place[slot, h] + n_ab, n_ab) * pairs
        i0 = first // occ
        turn = occ * (i0 + 1) - first
        raw = slots[slot, h, r0 : r0 + count, ks].astype(F32)
        right = rtab[pl.ds(pl.multiple_of(lax.rem(first, occ) + r0, 32), count), ks]
        pair = lax.broadcasted_iota(jnp.int32, (count, width), 0) + r0
        before, after = (jnp.concatenate([ltab[i, :, ks]] * (count // 8), axis=0) for i in (i0, i0 + 1))
        left = jnp.where(pair < turn, before, after)
        return (raw + left * right).astype(BF16)

    def product(parts, out, start=0, stop=None):
        total = sum(p[3] for p in parts)

        def piece(ks, width):
            formed = [tau(*p, ks, width) for p in parts]
            both = jnp.concatenate(formed, axis=0) if len(formed) > 1 else formed[0]
            return lax.dot_general(a_v[:, ks], both, (((1,), (1,)), ((), ())), preferred_element_type=F32)

        def step(t, carry):
            out[0:rows, 0:total] += piece(pl.ds(pl.multiple_of(t * KC, KC), KC), KC)
            return carry

        whole = cols // KC
        if stop is None:
            tail = piece(pl.ds(whole * KC, cols - whole * KC), cols - whole * KC)
            if start:
                out[0:rows, 0:total] += tail
            else:
                out[0:rows, 0:total] = tail
            lax.fori_loop(start, whole, step, 0)
        else:
            out[0:rows, 0:total] = piece(pl.ds(start * KC, KC), KC)
            lax.fori_loop(start + 1, stop, step, 0)

    def put(value, parts):
        lane0 = 0
        for slot, h, r0, count in parts:
            o_ref[first_k[slot, h], :, r0 : r0 + count] = value[0:take, lane0 : lane0 + count]
            lane0 += count

    def z_copy(s, k):
        to = lax.rem(z + k, N_Z)
        return remote(
            sbuf.at[s, to], rbuf.at[s, k - 1], z_s.at[s, k - 1], z_r.at[s, k - 1], {"cd": x_hi * N_Z + to}
        )

    def scatter(s):
        for j in range(n_cd):
            sbuf[s, j % N_Z, j // N_Z, :, :] = acc[j * take : j * take + 32, :].astype(sbuf.dtype)

        def send(k, carry):
            z_copy(s, k).start()
            return carry

        lax.fori_loop(1, N_Z, send, 0)

    def x_copy(s):
        return remote(xsend.at[s], xrecv.at[s], x_s.at[s], x_r.at[s], {"cd": (1 - x_hi) * N_Z + z})

    def gather(s):
        def arrive(k, carry):
            z_copy(s, k).wait_recv()
            return carry

        lax.fori_loop(1, N_Z, arrive, 0)
        for dst, xo in ((xsend, 1 - x_hi), (tot, x_hi)):
            total = sbuf[s, z, xo].astype(F32)
            for k in range(N_Z - 1):
                total = total + rbuf[s, k, xo].astype(F32)
            dst[s] = total

    def finish(s, parts):
        x_copy(s).wait_recv()
        put(tot[s] + xrecv[s], parts)

    order = [(x, k) for k in (4, 3, 5, 2, 6, 1, 7, 0) for x in (1, 0) if x or k]

    def all_copies(send, recv, ss, rs):
        copies = []
        for x, k in order:
            to = lax.rem(x_hi + x, n_x) * N_Z + lax.rem(z + k, N_Z)
            n = 2 * k + x - 1
            copies.append(remote(send.at[to], recv.at[n], ss.at[n], rs.at[n], {"cd": to}))
        return copies

    def all_sum(send, recv, copies):
        for copy in reversed(copies):
            copy.wait_recv()
        value = send[cd].astype(F32)
        for n in range(n_cd - 1):
            value = value + recv[n].astype(F32)
        return value

    acc[rows:, :] = jnp.zeros((acc.shape[0] - rows, acc.shape[1]), F32)
    acc_l[rows:, :] = jnp.zeros((acc_l.shape[0] - rows, acc_l.shape[1]), F32)

    parts = [
        [(0, 0, 0, pairs), (0, 1, 0, pairs)],
        [(1, 0, 0, half), (1, 1, half, half), (2, 0, 0, half), (2, 1, half, half)],
        [(1, 0, half, half), (1, 1, 0, half), (2, 0, half, half), (2, 1, 0, half)],
    ]
    late = [(3, 1, 0, pairs)]
    late_1 = [(3, 1, 0, pairs), (3, 0, 0, pairs)]
    last = [(3, 0, 0, pairs)]
    top = (take + 1) // 2

    load_d.wait()
    load_a.wait()
    own.wait_recv()
    product(parts[0], acc)
    scatter(0)

    sh_up_in = [remote(slots.at[1, 1 - core, q], slots.at[1, 1 - core, q], sib_s.at[i], sib_r.at[i], sib) for i, q in enumerate(other)]
    sh_dn_in = [remote(slots.at[2, 1 - core, q], slots.at[2, 1 - core, q], sib_s.at[2 + i], sib_r.at[2 + i], sib) for i, q in enumerate(other)]
    sh_f1_in = remote(slots.at[3, 1, part[0]], slots.at[3, 1, part[0]], sib_s.at[4], sib_r.at[4], sib)

    up[0].wait_recv()
    sh_up[0].start()
    dn[0].wait_recv()
    sh_dn[0].start()

    @pl.when(core == 0)
    def _():
        fd[0].start()

    sh_up_in[0].wait_recv()

    @pl.when(core == 0)
    def _():
        f1[0].start()
        f1[1].start()
        f0[0].start()
        f0[1].start()

    sh_dn_in[0].wait_recv()
    product(parts[1], acc)
    scatter(1)

    up[1].wait_recv()

    @pl.when(core == 1)
    def _():
        f1[0].start()

    up[2].wait_recv()
    sh_up[1].start()

    @pl.when(core == 1)
    def _():
        f1[1].start()

    dn[1].wait_recv()
    sh_dn[1].start()

    @pl.when(core == 0)
    def _():
        fd[1].start()

    sh_up_in[1].wait_recv()

    @pl.when(core == 1)
    def _():
        f0[0].start()
        f0[1].start()

    sh_dn_in[1].wait_recv()
    product(parts[2], acc)
    scatter(2)
    gather(0)
    gather(1)

    f1[0].wait_recv()
    f1[1].wait_recv()
    sh_f1.start()
    gather(2)
    l_copies = all_copies(lsend, lrecv, l_s, l_r)

    @pl.when(core == 0)
    def _():
        sh_f1_in.wait_recv()
        product(late, acc)

    @pl.when(core == 1)
    def _():
        fd_in[0].wait_recv()
        fd_in[1].wait_recv()
        sh_f1_in.wait_recv()
        product(late_1, acc)

    scatter(3)

    @pl.when(core == 0)
    def _():
        for copy in f0_in[0]:
            copy.wait_recv()
        product(last, acc_l, 0, CUT // KC)
        for copy in f0_in[1]:
            copy.wait_recv()
        product(last, acc_l, CUT // KC)
        for j in range(n_cd):
            halves = [acc_l[j * take + r : j * take + r + 16, :] for r in (0, top)]
            lsend[j, :, :] = jnp.concatenate(halves, axis=1).astype(lsend.dtype)
        for copy in l_copies:
            copy.start()

    f0[1].wait_send()
    for s in range(3):
        x_copy(s).start()
    gather(3)
    x_copy(3).start()
    for s in range(3):
        finish(s, parts[s])
    finish(3, late)

    @pl.when(core == 1)
    def _():
        o_ref[first_k[3, 0], :, :] = (tot[3] + xrecv[3])[0:take, pairs : 2 * pairs]

    @pl.when(core == 0)
    def _():
        final = all_sum(lsend, lrecv, l_copies)
        o_ref[first_k[3, 0], 0:top, :] = final[0:top, 0:pairs]
        o_ref[first_k[3, 0], top:take, :] = final[0 : take - top, pairs : 2 * pairs]

    for copy in (*up, *dn, own, *sh_up, *sh_dn, *f1, sh_f1, f0[0]):
        copy.wait_send()

    @pl.when(core == 0)
    def _():
        for copy in (*fd, *l_copies):
            copy.wait_send()

    for s in range(4):
        x_copy(s).wait_send()

        def sent(k, carry, s=s):
            z_copy(s, k).wait_send()
            return carry

        lax.fori_loop(1, N_Z, sent, 0)


def shards(integrals, doubles, singles):
    rows, cols = integrals.shape
    pairs = doubles.shape[0]
    occ, virt = singles.shape
    n_ab, n_cd = lax.axis_size("ab"), lax.axis_size("cd")
    steps = n_ab // 4
    take = rows // n_cd
    dma = pltpu.SemaphoreType.DMA
    return pl.pallas_call(
        kernel,
        out_shape=jax.ShapeDtypeStruct((steps, take, pairs), F32),
        in_specs=[pl.BlockSpec(memory_space=pl.ANY)] * 3,
        out_specs=pl.BlockSpec(memory_space=pltpu.VMEM),
        scratch_shapes=[
            pltpu.VMEM((rows, cols), BF16),
            pltpu.VMEM((occ, virt), F32),
            pltpu.VMEM((4, 2, pairs, cols), BF16),
            pltpu.VMEM((occ + 32, cols), F32),
            pltpu.VMEM((16, 8, cols), F32),
            pltpu.VMEM((rows + 8, 2 * pairs), F32),
            pltpu.VMEM((rows + 8, pairs), F32),
            pltpu.VMEM((4, N_Z, n_cd // N_Z, 32, 2 * pairs), BF16),
            pltpu.VMEM((4, N_Z - 1, n_cd // N_Z, 32, 2 * pairs), BF16),
            pltpu.VMEM((4, 32, 2 * pairs), F32),
            pltpu.VMEM((4, 32, 2 * pairs), F32),
            pltpu.VMEM((4, 32, 2 * pairs), F32),
            pltpu.VMEM((n_cd, 16, 2 * pairs), BF16),
            pltpu.VMEM((n_cd - 1, 16, 2 * pairs), BF16),
            dma((3,)),
            dma((3,)), dma((3,)), dma((2,)), dma((2,)), dma((2,)), dma((2,)),
            dma((2,)), dma((2,)), dma((2,)), dma((2, 2)),
            dma((6,)), dma((6,)),
            dma((4, N_Z - 1)), dma((4, N_Z - 1)),
            dma((4,)), dma((4,)),
            dma((n_cd - 1,)), dma((n_cd - 1,)),
        ],
        compiler_params=pltpu.CompilerParams(
            collective_id=0, has_side_effects=True, vmem_limit_bytes=60 * 2**20
        ),
        cost_estimate=pl.CostEstimate(
            flops=2 * rows * cols * steps * pairs, bytes_accessed=2 * (rows + pairs) * cols, transcendentals=0
        ),
    )(integrals, doubles, singles)


def solution(mesh):
    in_specs = (P("ab", "cd"), P("ab", "cd"), P())
    out_specs = P(None, ("ab", "cd"), None)
    return jax.shard_map(shards, mesh=mesh, in_specs=in_specs, out_specs=out_specs, check_vma=False)
```

```python
import functools

import jax
import jax.numpy as jnp
from jax import lax
from jax.experimental import pallas as pl
from jax.experimental.pallas import tpu as pltpu
from jax.sharding import PartitionSpec as P

MESH = pl.DeviceIdType.MESH
F32 = jnp.float32
BF16 = jnp.bfloat16
N_Z = 8
KC = 1024
VMEM_GRANT = 53 * 2**20 + 704 * 2**10
CUT = 4096


def kernel(
    a_hbm, d_hbm, s_hbm, o_ref,
    a_v, s_v, slots, rtab, ltab, acc, acc_l,
    sbuf, rbuf, xsend, xrecv, tot, lsend, lrecv,
    loc_sem, up_s, up_r, dn_s, dn_r, fd_s, fd_r, f1_s, f1_r, f0_s, f0_r, sib_s, sib_r,
    z_s, z_r, x_s, x_r, l_s, l_r,
):
    pairs, cols = d_hbm.shape
    rows = a_hbm.shape[0]
    occ, virt = s_hbm.shape
    c_local = cols // virt
    n_ab = lax.axis_size("ab")
    n_cd = lax.axis_size("cd")
    n_x = n_cd // N_Z
    take = rows // n_cd
    half = pairs // 2

    ab = lax.axis_index("ab")
    cd = lax.axis_index("cd")
    core = lax.rem(ab, 2)
    chip2 = ab - core
    x_hi = cd // N_Z
    z = lax.rem(cd, N_Z)

    nxt = {"ab": lax.rem(ab + 2, n_ab)}
    prv = {"ab": lax.rem(ab + n_ab - 2, n_ab)}
    sib = {"ab": ab + 1 - 2 * core}
    low = {"ab": lax.rem(ab + n_ab - 1, n_ab)}
    high = {"ab": lax.rem(ab + 1, n_ab)}
    nxt0 = {"ab": lax.rem(chip2 + 2, n_ab)}

    bar = pltpu.get_barrier_semaphore()
    for peer in (nxt, prv, low, high):
        pl.semaphore_signal(bar, inc=1, device_id=peer, device_id_type=MESH)

    def greet(k, carry):
        pl.semaphore_signal(bar, inc=1, device_id={"cd": lax.rem(cd + k, n_cd)}, device_id_type=MESH)
        return carry

    lax.fori_loop(1, n_cd, greet, 0)

    load_s = pltpu.make_async_copy(s_hbm, s_v, loc_sem.at[0])
    load_d = pltpu.make_async_copy(d_hbm, slots.at[0, core], loc_sem.at[1])
    load_a = pltpu.make_async_copy(a_hbm, a_v, loc_sem.at[2])
    load_s.start()
    load_d.start()
    load_a.start()

    pl.semaphore_wait(bar, n_cd + 3)

    def remote(src, dst, ss, rs, dev):
        return pltpu.make_async_remote_copy(
            src_ref=src, dst_ref=dst, send_sem=ss, recv_sem=rs, device_id=dev, device_id_type=MESH
        )

    part = [pl.ds(pl.multiple_of(half * r, 32), half) for r in (core, 1 - core)]
    other = [pl.ds(pl.multiple_of(half * r, 32), half) for r in (1 - core, core)]
    quarter = half // 2
    halved = [pl.ds(pl.multiple_of(half * (1 - core) + quarter * j, 16), quarter) for j in range(2)]
    up_rows = [part[0], *halved]
    up = [remote(d_hbm.at[q], slots.at[1, core, q], up_s.at[i], up_r.at[i], nxt) for i, q in enumerate(up_rows)]
    dn = [remote(d_hbm.at[q], slots.at[2, core, q], dn_s.at[i], dn_r.at[i], prv) for i, q in enumerate(part)]
    own = remote(d_hbm, slots.at[0, core], sib_s.at[5], sib_r.at[5], sib)
    sh_up = [remote(slots.at[1, core, q], slots.at[1, core, q], sib_s.at[i], sib_r.at[i], sib) for i, q in enumerate(part)]
    sh_dn = [remote(slots.at[2, core, q], slots.at[2, core, q], sib_s.at[2 + i], sib_r.at[2 + i], sib) for i, q in enumerate(part)]
    f1 = [remote(slots.at[1, 1, q], slots.at[3, 1, q], f1_s.at[j], f1_r.at[j], nxt) for j, q in enumerate(halved)]
    sh_f1 = remote(slots.at[3, 1, part[1]], slots.at[3, 1, part[1]], sib_s.at[4], sib_r.at[4], sib)
    spans = [pl.ds(0, CUT), pl.ds(CUT, cols - CUT)]
    f0 = [
        remote(slots.at[1, 0, part[0], c], slots.at[3, 0, part[0], c], f0_s.at[j], f0_r.at[core, j], nxt0)
        for j, c in enumerate(spans)
    ]
    f0_in = [
        [
            remote(slots.at[1, 0, q, c], slots.at[3, 0, q, c], f0_s.at[j], f0_r.at[i, j], nxt0)
            for i, q in enumerate((pl.ds(0, half), pl.ds(half, half)))
        ]
        for j, c in enumerate(spans)
    ]
    fd = [remote(slots.at[2, core, q], slots.at[3, core, q], fd_s.at[i], fd_r.at[i], low) for i, q in enumerate(part)]
    fd_in = [remote(slots.at[2, 0, q], slots.at[3, 0, q], fd_s.at[i], fd_r.at[i], low) for i, q in enumerate(other)]

    up[0].start()
    dn[0].start()
    own.start()
    up[1].start()
    up[2].start()
    dn[1].start()

    load_s.wait()

    def spread(t, carry):
        rows_t = s_v[pl.ds(pl.multiple_of(lax.rem(32 * t, occ), 32), 32), :]
        at = pl.ds(pl.multiple_of(32 * t, 32), 32)
        for c in range(c_local):
            rtab[at, c * virt : (c + 1) * virt] = rows_t
        return carry

    lax.fori_loop(0, rtab.shape[0] // 32, spread, 0)
    few = s_v[0 : ltab.shape[0], :]
    lane = lax.broadcasted_iota(jnp.int32, few.shape, 1)
    for c in range(c_local):
        value = jnp.sum(jnp.where(lane == cd * c_local + c, few, 0.0), axis=1, keepdims=True)
        for i in range(few.shape[0]):
            ltab[i, :, c * virt : (c + 1) * virt] = jnp.broadcast_to(value[i : i + 1, :], (8, virt))

    far = jnp.where(core == 0, -4, 4)
    place = {(0, 0): 0, (0, 1): 1, (1, 0): -2, (1, 1): -1, (2, 0): 2, (2, 1): 3, (3, 0): far, (3, 1): -3}
    first_k = {
        (0, 0): 3 + core, (0, 1): 2 + core, (1, 0): 5 + core, (1, 1): 4 + core,
        (2, 0): 1 + core, (2, 1): core, (3, 0): 7 - 7 * core, (3, 1): 6 + core,
    }

    def tau(slot, h, r0, count, ks, width):
        first = lax.rem(chip2 + place[slot, h] + n_ab, n_ab) * pairs
        i0 = first // occ
        turn = occ * (i0 + 1) - first
        raw = slots[slot, h, r0 : r0 + count, ks].astype(F32)
        right = rtab[pl.ds(pl.multiple_of(lax.rem(first, occ) + r0, 32), count), ks]
        pair = lax.broadcasted_iota(jnp.int32, (count, width), 0) + r0
        before, after = (jnp.concatenate([ltab[i, :, ks]] * (count // 8), axis=0) for i in (i0, i0 + 1))
        left = jnp.where(pair < turn, before, after)
        return (raw + left * right).astype(BF16)

    def product(parts, out, start=0, stop=None):
        total = sum(p[3] for p in parts)

        def piece(ks, width):
            formed = [tau(*p, ks, width) for p in parts]
            both = jnp.concatenate(formed, axis=0) if len(formed) > 1 else formed[0]
            return lax.dot_general(a_v[:, ks], both, (((1,), (1,)), ((), ())), preferred_element_type=F32)

        def step(t, carry):
            out[0:rows, 0:total] += piece(pl.ds(pl.multiple_of(t * KC, KC), KC), KC)
            return carry

        whole = cols // KC
        if stop is None:
            tail = piece(pl.ds(whole * KC, cols - whole * KC), cols - whole * KC)
            if start:
                out[0:rows, 0:total] += tail
            else:
                out[0:rows, 0:total] = tail
            lax.fori_loop(start, whole, step, 0)
        else:
            out[0:rows, 0:total] = piece(pl.ds(start * KC, KC), KC)
            lax.fori_loop(start + 1, stop, step, 0)

    def put(value, parts):
        lane0 = 0
        for slot, h, r0, count in parts:
            o_ref[first_k[slot, h], :, r0 : r0 + count] = value[0:take, lane0 : lane0 + count]
            lane0 += count

    def z_copy(s, k):
        to = lax.rem(z + k, N_Z)
        return remote(
            sbuf.at[s, to], rbuf.at[s, k - 1], z_s.at[s, k - 1], z_r.at[s, k - 1], {"cd": x_hi * N_Z + to}
        )

    def scatter(s):
        for j in range(n_cd):
            sbuf[s, j % N_Z, j // N_Z, :, :] = acc[j * take : j * take + 32, :].astype(sbuf.dtype)

        for k in (4, 3, 5, 2, 6, 1, 7):
            z_copy(s, k).start()

    def x_copy(s):
        return remote(xsend.at[s], xrecv.at[s], x_s.at[s], x_r.at[s], {"cd": (1 - x_hi) * N_Z + z})

    def gather(s):
        def arrive(k, carry):
            z_copy(s, k).wait_recv()
            return carry

        lax.fori_loop(1, N_Z, arrive, 0)
        for dst, xo in ((xsend, 1 - x_hi), (tot, x_hi)):
            total = sbuf[s, z, xo].astype(F32)
            for k in range(N_Z - 1):
                total = total + rbuf[s, k, xo].astype(F32)
            dst[s] = total

    def finish(s, parts):
        x_copy(s).wait_recv()
        put(tot[s] + xrecv[s], parts)

    order = [(x, k) for k in (4, 3, 5, 2, 6, 1, 7, 0) for x in (1, 0) if x or k]

    def all_copies(send, recv, ss, rs):
        copies = []
        for x, k in order:
            to = lax.rem(x_hi + x, n_x) * N_Z + lax.rem(z + k, N_Z)
            n = 2 * k + x - 1
            copies.append(remote(send.at[to], recv.at[n], ss.at[n], rs.at[n], {"cd": to}))
        return copies

    def all_sum(send, recv, copies):
        for copy in reversed(copies):
            copy.wait_recv()
        value = send[cd].astype(F32)
        for n in range(n_cd - 1):
            value = value + recv[n].astype(F32)
        return value

    acc[rows:, :] = jnp.zeros((acc.shape[0] - rows, acc.shape[1]), F32)
    acc_l[rows:, :] = jnp.zeros((acc_l.shape[0] - rows, acc_l.shape[1]), F32)

    parts = [
        [(0, 0, 0, pairs), (0, 1, 0, pairs)],
        [(1, 0, 0, half), (1, 1, half, half), (2, 0, 0, half), (2, 1, half, half)],
        [(1, 0, half, half), (1, 1, 0, half), (2, 0, half, half), (2, 1, 0, half)],
    ]
    late = [(3, 1, 0, pairs)]
    late_1 = [(3, 1, 0, pairs), (3, 0, 0, pairs)]
    last = [(3, 0, 0, pairs)]
    top = (take + 1) // 2

    load_d.wait()
    load_a.wait()
    own.wait_recv()
    product(parts[0], acc)
    scatter(0)

    sh_up_in = [remote(slots.at[1, 1 - core, q], slots.at[1, 1 - core, q], sib_s.at[i], sib_r.at[i], sib) for i, q in enumerate(other)]
    sh_dn_in = [remote(slots.at[2, 1 - core, q], slots.at[2, 1 - core, q], sib_s.at[2 + i], sib_r.at[2 + i], sib) for i, q in enumerate(other)]
    sh_f1_in = remote(slots.at[3, 1, part[0]], slots.at[3, 1, part[0]], sib_s.at[4], sib_r.at[4], sib)

    up[0].wait_recv()
    sh_up[0].start()
    dn[0].wait_recv()
    sh_dn[0].start()

    @pl.when(core == 0)
    def _():
        fd[0].start()

    sh_up_in[0].wait_recv()

    @pl.when(core == 0)
    def _():
        f1[0].start()
        f1[1].start()
        f0[0].start()
        f0[1].start()

    sh_dn_in[0].wait_recv()
    product(parts[1], acc)
    scatter(1)

    up[1].wait_recv()

    @pl.when(core == 1)
    def _():
        f1[0].start()

    up[2].wait_recv()
    sh_up[1].start()

    @pl.when(core == 1)
    def _():
        f1[1].start()

    dn[1].wait_recv()
    sh_dn[1].start()

    @pl.when(core == 0)
    def _():
        fd[1].start()

    sh_up_in[1].wait_recv()

    @pl.when(core == 1)
    def _():
        f0[0].start()
        f0[1].start()

    sh_dn_in[1].wait_recv()
    product(parts[2], acc)
    scatter(2)
    gather(0)
    gather(1)

    f1[0].wait_recv()
    f1[1].wait_recv()
    sh_f1.start()
    l_copies = all_copies(lsend, lrecv, l_s, l_r)

    @pl.when(core == 0)
    def _():
        sh_f1_in.wait_recv()
        product(late, acc)

    @pl.when(core == 1)
    def _():
        fd_in[0].wait_recv()
        fd_in[1].wait_recv()
        sh_f1_in.wait_recv()
        product(late_1, acc)

    scatter(3)
    gather(2)

    @pl.when(core == 0)
    def _():
        for copy in f0_in[0]:
            copy.wait_recv()
        product(last, acc_l, 0, CUT // KC)
        for copy in f0_in[1]:
            copy.wait_recv()
        product(last, acc_l, CUT // KC)
        for j in range(n_cd):
            halves = [acc_l[j * take + r : j * take + r + 16, :] for r in (0, top)]
            lsend[j, :, :] = jnp.concatenate(halves, axis=1).astype(lsend.dtype)
        for copy in l_copies:
            copy.start()

    f0[1].wait_send()
    for s in range(3):
        x_copy(s).start()
    gather(3)
    x_copy(3).start()

    for copy in (*up, *dn, own, *sh_up, *sh_dn, *f1, sh_f1, f0[0]):
        copy.wait_send()

    @pl.when(core == 0)
    def _():
        for copy in (*fd, *l_copies):
            copy.wait_send()

    for s in range(4):

        def sent(k, carry, s=s):
            z_copy(s, k).wait_send()
            return carry

        lax.fori_loop(1, N_Z, sent, 0)
    for s in range(3):
        finish(s, parts[s])
    finish(3, late)
    for s in range(4):
        x_copy(s).wait_send()

    @pl.when(core == 1)
    def _():
        o_ref[first_k[3, 0], :, :] = (tot[3] + xrecv[3])[0:take, pairs : 2 * pairs]

    @pl.when(core == 0)
    def _():
        final = all_sum(lsend, lrecv, l_copies)
        o_ref[first_k[3, 0], 0:top, :] = final[0:top, 0:pairs]
        o_ref[first_k[3, 0], top:take, :] = final[0 : take - top, pairs : 2 * pairs]


def shards(integrals, doubles, singles):
    rows, cols = integrals.shape
    pairs = doubles.shape[0]
    occ, virt = singles.shape
    n_ab, n_cd = lax.axis_size("ab"), lax.axis_size("cd")
    steps = n_ab // 4
    take = rows // n_cd
    dma = pltpu.SemaphoreType.DMA
    return pl.pallas_call(
        kernel,
        out_shape=jax.ShapeDtypeStruct((steps, take, pairs), F32),
        in_specs=[pl.BlockSpec(memory_space=pl.ANY)] * 3,
        out_specs=pl.BlockSpec(memory_space=pltpu.VMEM),
        scratch_shapes=[
            pltpu.VMEM((rows, cols), BF16),
            pltpu.VMEM((occ, virt), F32),
            pltpu.VMEM((4, 2, pairs, cols), BF16),
            pltpu.VMEM((occ + 32, cols), F32),
            pltpu.VMEM((16, 8, cols), F32),
            pltpu.VMEM((rows + 8, 2 * pairs), F32),
            pltpu.VMEM((rows + 8, pairs), F32),
            pltpu.VMEM((4, N_Z, n_cd // N_Z, 32, 2 * pairs), BF16),
            pltpu.VMEM((4, N_Z - 1, n_cd // N_Z, 32, 2 * pairs), BF16),
            pltpu.VMEM((4, 32, 2 * pairs), F32),
            pltpu.VMEM((4, 32, 2 * pairs), F32),
            pltpu.VMEM((4, 32, 2 * pairs), F32),
            pltpu.VMEM((n_cd, 16, 2 * pairs), BF16),
            pltpu.VMEM((n_cd - 1, 16, 2 * pairs), BF16),
            dma((3,)),
            dma((3,)), dma((3,)), dma((2,)), dma((2,)), dma((2,)), dma((2,)),
            dma((2,)), dma((2,)), dma((2,)), dma((2, 2)),
            dma((6,)), dma((6,)),
            dma((4, N_Z - 1)), dma((4, N_Z - 1)),
            dma((4,)), dma((4,)),
            dma((n_cd - 1,)), dma((n_cd - 1,)),
        ],
        compiler_params=pltpu.CompilerParams(
            collective_id=0, has_side_effects=True, vmem_limit_bytes=VMEM_GRANT
        ),
        cost_estimate=pl.CostEstimate(
            flops=2 * rows * cols * steps * pairs, bytes_accessed=2 * (rows + pairs) * cols, transcendentals=0
        ),
    )(integrals, doubles, singles)


def solution(mesh):
    in_specs = (P("ab", "cd"), P("ab", "cd"), P())
    out_specs = P(None, ("ab", "cd"), None)
    return jax.shard_map(shards, mesh=mesh, in_specs=in_specs, out_specs=out_specs, check_vma=False)
```

```python
import functools

import jax
import jax.numpy as jnp
from jax import lax
from jax.experimental import pallas as pl
from jax.experimental.pallas import tpu as pltpu
from jax.sharding import PartitionSpec as P

MESH = pl.DeviceIdType.MESH
F32 = jnp.float32
BF16 = jnp.bfloat16
N_Z = 8
KC = 2048
VMEM_GRANT = 53 * 2**20 + 704 * 2**10
CUTS = (0, 2048, 4096)


def kernel(
    a_hbm, d_hbm, s_hbm, o_ref,
    a_v, s_v, slots, rtab, ltab, acc, acc_l,
    sbuf, rbuf, xsend, xrecv, tot, lsend, lrecv,
    loc_sem, up_s, up_r, dn_s, dn_r, fd_s, fd_r, f1_s, f1_r, f0_s, f0_r, sib_s, sib_r,
    z_s, z_r, x_s, x_r, l_s, l_r,
):
    pairs, cols = d_hbm.shape
    rows = a_hbm.shape[0]
    occ, virt = s_hbm.shape
    c_local = cols // virt
    n_ab = lax.axis_size("ab")
    n_cd = lax.axis_size("cd")
    n_x = n_cd // N_Z
    take = rows // n_cd
    half = pairs // 2

    ab = lax.axis_index("ab")
    cd = lax.axis_index("cd")
    core = lax.rem(ab, 2)
    chip2 = ab - core
    x_hi = cd // N_Z
    z = lax.rem(cd, N_Z)

    nxt = {"ab": lax.rem(ab + 2, n_ab)}
    prv = {"ab": lax.rem(ab + n_ab - 2, n_ab)}
    sib = {"ab": ab + 1 - 2 * core}
    low = {"ab": lax.rem(ab + n_ab - 1, n_ab)}
    high = {"ab": lax.rem(ab + 1, n_ab)}
    nxt0 = {"ab": lax.rem(chip2 + 2, n_ab)}

    bar = pltpu.get_barrier_semaphore()
    for peer in (nxt, prv, low, high):
        pl.semaphore_signal(bar, inc=1, device_id=peer, device_id_type=MESH)

    def greet(k, carry):
        pl.semaphore_signal(bar, inc=1, device_id={"cd": lax.rem(cd + k, n_cd)}, device_id_type=MESH)
        return carry

    lax.fori_loop(1, n_cd, greet, 0)

    load_s = pltpu.make_async_copy(s_hbm, s_v, loc_sem.at[0])
    load_d = pltpu.make_async_copy(d_hbm, slots.at[0, core], loc_sem.at[1])
    load_a = pltpu.make_async_copy(a_hbm, a_v, loc_sem.at[2])
    load_d.start()
    load_s.start()
    load_a.start()

    pl.semaphore_wait(bar, n_cd + 3)

    def remote(src, dst, ss, rs, dev):
        return pltpu.make_async_remote_copy(
            src_ref=src, dst_ref=dst, send_sem=ss, recv_sem=rs, device_id=dev, device_id_type=MESH
        )

    part = [pl.ds(pl.multiple_of(half * r, 32), half) for r in (core, 1 - core)]
    other = [pl.ds(pl.multiple_of(half * r, 32), half) for r in (1 - core, core)]
    quarter = half // 2
    halved = [pl.ds(pl.multiple_of(half * (1 - core) + quarter * j, 16), quarter) for j in range(2)]
    up_rows = [part[0], *halved]
    up = [remote(slots.at[0, core, q], slots.at[1, core, q], up_s.at[i], up_r.at[i], nxt) for i, q in enumerate(up_rows)]
    dn = [remote(slots.at[0, core, q], slots.at[2, core, q], dn_s.at[i], dn_r.at[i], prv) for i, q in enumerate(part)]
    own = remote(slots.at[0, core], slots.at[0, core], sib_s.at[5], sib_r.at[5], sib)
    sh_up = [remote(slots.at[1, core, q], slots.at[1, core, q], sib_s.at[i], sib_r.at[i], sib) for i, q in enumerate(part)]
    sh_dn = [remote(slots.at[2, core, q], slots.at[2, core, q], sib_s.at[2 + i], sib_r.at[2 + i], sib) for i, q in enumerate(part)]
    f1 = [remote(slots.at[1, 1, q], slots.at[3, 1, q], f1_s.at[j], f1_r.at[j], nxt) for j, q in enumerate(halved)]
    sh_f1 = [remote(slots.at[3, 1, q], slots.at[3, 1, q], sib_s.at[j], sib_r.at[j], sib) for j, q in zip((4, 6), halved)]
    ends = (*CUTS[1:], cols)
    spans = [pl.ds(a, b - a) for a, b in zip(CUTS, ends)]
    f0 = [
        remote(slots.at[1, 0, part[0], c], slots.at[3, 0, part[0], c], f0_s.at[j], f0_r.at[core, j], nxt0)
        for j, c in enumerate(spans)
    ]
    f0_in = [
        [
            remote(slots.at[1, 0, q, c], slots.at[3, 0, q, c], f0_s.at[j], f0_r.at[i, j], nxt0)
            for i, q in enumerate((pl.ds(0, half), pl.ds(half, half)))
        ]
        for j, c in enumerate(spans)
    ]
    fd = [remote(slots.at[2, core, q], slots.at[3, core, q], fd_s.at[i], fd_r.at[i], low) for i, q in enumerate(part)]
    fd_in = [remote(slots.at[2, 0, q], slots.at[3, 0, q], fd_s.at[i], fd_r.at[i], low) for i, q in enumerate(other)]

    load_d.wait()
    up[0].start()
    dn[0].start()
    own.start()
    up[1].start()
    up[2].start()
    dn[1].start()

    load_s.wait()

    def spread(t, carry):
        rows_t = s_v[pl.ds(pl.multiple_of(lax.rem(32 * t, occ), 32), 32), :]
        at = pl.ds(pl.multiple_of(32 * t, 32), 32)
        for c in range(c_local):
            rtab[at, c * virt : (c + 1) * virt] = rows_t
        return carry

    lax.fori_loop(0, rtab.shape[0] // 32, spread, 0)
    few = s_v[0 : ltab.shape[0], :]
    lane = lax.broadcasted_iota(jnp.int32, few.shape, 1)
    for c in range(c_local):
        value = jnp.sum(jnp.where(lane == cd * c_local + c, few, 0.0), axis=1, keepdims=True)
        for i in range(few.shape[0]):
            ltab[i, :, c * virt : (c + 1) * virt] = jnp.broadcast_to(value[i : i + 1, :], (8, virt))

    far = jnp.where(core == 0, -4, 4)
    place = {(0, 0): 0, (0, 1): 1, (1, 0): -2, (1, 1): -1, (2, 0): 2, (2, 1): 3, (3, 0): far, (3, 1): -3}
    row = lax.rem(ab // 2, n_ab // 4)
    inner = jnp.logical_and(row > 0, row < n_ab // 4 - 1)
    first_k = {
        (0, 0): 3 + core, (0, 1): 2 + core, (1, 0): 5 + core, (1, 1): 4 + core,
        (2, 0): 1 + core, (2, 1): core, (3, 0): 7 - 7 * core, (3, 1): 6 + core,
    }

    def tau(slot, h, r0, count, ks, width):
        first = lax.rem(chip2 + place[slot, h] + n_ab, n_ab) * pairs
        i0 = first // occ
        turn = occ * (i0 + 1) - first
        raw = slots[slot, h, r0 : r0 + count, ks].astype(F32)
        right = rtab[pl.ds(pl.multiple_of(lax.rem(first, occ) + r0, 32), count), ks]
        pair = lax.broadcasted_iota(jnp.int32, (count, width), 0) + r0
        before, after = (jnp.concatenate([ltab[i, :, ks]] * (count // 8), axis=0) for i in (i0, i0 + 1))
        left = jnp.where(pair < turn, before, after)
        return (raw + left * right).astype(BF16)

    def product(parts, out, start=0, stop=None):
        total = sum(p[3] for p in parts)

        def piece(ks, width):
            formed = [tau(*p, ks, width) for p in parts]
            both = jnp.concatenate(formed, axis=0) if len(formed) > 1 else formed[0]
            return lax.dot_general(a_v[:, ks], both, (((1,), (1,)), ((), ())), preferred_element_type=F32)

        def step(t, carry):
            out[0:rows, 0:total] += piece(pl.ds(pl.multiple_of(t * KC, KC), KC), KC)
            return carry

        whole = cols // KC
        if stop is None:
            tail = piece(pl.ds(whole * KC, cols - whole * KC), cols - whole * KC)
            if start:
                out[0:rows, 0:total] += tail
            else:
                out[0:rows, 0:total] = tail
            lax.fori_loop(start, whole, step, 0)
        else:
            if start == 0:
                out[0:rows, 0:total] = piece(pl.ds(0, KC), KC)
            lax.fori_loop(max(start, 1), stop, step, 0)

    def put(value, parts):
        lane0 = 0
        for slot, h, r0, count in parts:
            o_ref[first_k[slot, h], :, r0 : r0 + count] = value[0:take, lane0 : lane0 + count]
            lane0 += count

    def z_copy(s, k):
        to = lax.rem(z + k, N_Z)
        return remote(
            sbuf.at[s, to], rbuf.at[s, k - 1], z_s.at[s, k - 1], z_r.at[s, k - 1], {"cd": x_hi * N_Z + to}
        )

    def scatter(s):
        for j in range(n_cd):
            sbuf[s, j % N_Z, j // N_Z, :, :] = acc[j * take : j * take + 32, :].astype(sbuf.dtype)

        for k in (4, 3, 5, 2, 6, 1, 7):
            z_copy(s, k).start()

    def x_copy(s):
        return remote(xsend.at[s], xrecv.at[s], x_s.at[s], x_r.at[s], {"cd": (1 - x_hi) * N_Z + z})

    def gather(s):
        def arrive(k, carry):
            z_copy(s, k).wait_recv()
            return carry

        lax.fori_loop(1, N_Z, arrive, 0)
        for dst, xo in ((xsend, 1 - x_hi), (tot, x_hi)):
            total = sbuf[s, z, xo].astype(F32)
            for k in range(N_Z - 1):
                total = total + rbuf[s, k, xo].astype(F32)
            dst[s] = total

        @pl.when(jnp.logical_and(inner, s < 3))
        def _():
            x_copy(s).start()

    def finish(s, parts):
        x_copy(s).wait_recv()
        put(tot[s] + xrecv[s], parts)

    order = [(x, k) for k in (4, 3, 5, 2, 6, 1, 7, 0) for x in (1, 0) if x or k]

    def all_copies(send, recv, ss, rs):
        copies = []
        for x, k in order:
            to = lax.rem(x_hi + x, n_x) * N_Z + lax.rem(z + k, N_Z)
            n = 2 * k + x - 1
            copies.append(remote(send.at[to], recv.at[n], ss.at[n], rs.at[n], {"cd": to}))
        return copies

    def all_sum(send, recv, copies):
        for copy in reversed(copies):
            copy.wait_recv()
        value = send[cd].astype(F32)
        for n in range(n_cd - 1):
            value = value + recv[n].astype(F32)
        return value

    acc[rows:, :] = jnp.zeros((acc.shape[0] - rows, acc.shape[1]), F32)
    acc_l[rows:, :] = jnp.zeros((acc_l.shape[0] - rows, acc_l.shape[1]), F32)

    parts = [
        [(0, 0, 0, pairs), (0, 1, 0, pairs)],
        [(1, 0, 0, half), (1, 1, half, half), (2, 0, 0, half), (2, 1, half, half)],
        [(1, 0, half, half), (1, 1, 0, half), (2, 0, half, half), (2, 1, 0, half)],
    ]
    late = [(3, 1, 0, pairs)]
    late_1 = [(3, 1, 0, pairs), (3, 0, 0, pairs)]
    last = [(3, 0, 0, pairs)]
    top = (take + 1) // 2

    load_a.wait()
    own.wait_recv()
    product(parts[0], acc)
    scatter(0)

    sh_up_in = [remote(slots.at[1, 1 - core, q], slots.at[1, 1 - core, q], sib_s.at[i], sib_r.at[i], sib) for i, q in enumerate(other)]
    sh_dn_in = [remote(slots.at[2, 1 - core, q], slots.at[2, 1 - core, q], sib_s.at[2 + i], sib_r.at[2 + i], sib) for i, q in enumerate(other)]
    theirs = [pl.ds(pl.multiple_of(half * core + quarter * j, 16), quarter) for j in range(2)]
    sh_f1_in = [remote(slots.at[3, 1, q], slots.at[3, 1, q], sib_s.at[j], sib_r.at[j], sib) for j, q in zip((4, 6), theirs)]

    up[0].wait_recv()
    sh_up[0].start()
    dn[0].wait_recv()
    sh_dn[0].start()

    @pl.when(core == 0)
    def _():
        fd[0].start()

    sh_up_in[0].wait_recv()

    @pl.when(core == 0)
    def _():
        f1[0].start()
        f1[1].start()
        for copy in f0:
            copy.start()

    sh_dn_in[0].wait_recv()
    product(parts[1], acc)
    scatter(1)

    up[1].wait_recv()

    @pl.when(core == 1)
    def _():
        f1[0].start()

    up[2].wait_recv()
    sh_up[1].start()

    @pl.when(core == 1)
    def _():
        f1[1].start()

    dn[1].wait_recv()
    sh_dn[1].start()

    @pl.when(core == 0)
    def _():
        fd[1].start()

    sh_up_in[1].wait_recv()

    @pl.when(core == 1)
    def _():
        for copy in f0:
            copy.start()

    sh_dn_in[1].wait_recv()
    product(parts[2], acc)
    scatter(2)
    gather(0)
    gather(1)

    for j in range(2):
        f1[j].wait_recv()
        sh_f1[j].start()
    l_copies = all_copies(lsend, lrecv, l_s, l_r)

    @pl.when(core == 0)
    def _():
        for copy in sh_f1_in:
            copy.wait_recv()
        product(late, acc)

    @pl.when(core == 1)
    def _():
        fd_in[0].wait_recv()
        fd_in[1].wait_recv()
        for copy in sh_f1_in:
            copy.wait_recv()
        product(late_1, acc)

    scatter(3)
    gather(2)

    @pl.when(core == 0)
    def _():
        for j, copies in enumerate(f0_in):
            for copy in copies:
                copy.wait_recv()
            product(last, acc_l, CUTS[j] // KC, ends[j] // KC if j + 1 < len(CUTS) else None)
        for j in range(n_cd):
            halves = [acc_l[j * take + r : j * take + r + 16, :] for r in (0, top)]
            lsend[j, :, :] = jnp.concatenate(halves, axis=1).astype(lsend.dtype)
        def send(t, carry):
            x = n_x - 1 - lax.rem(t, n_x)
            k = lax.rem(t // n_x - z + N_Z, N_Z)

            @pl.when(x + k > 0)
            def _():
                to = lax.rem(x_hi + x, n_x) * N_Z + t // n_x
                n = n_x * k + x - 1
                remote(lsend.at[to], lrecv.at[n], l_s.at[n], l_r.at[n], {"cd": to}).start()

            return carry

        lax.fori_loop(0, n_cd, send, 0)

    for copy in f0:
        copy.wait_send()

    @pl.when(jnp.logical_not(inner))
    def _():
        for s in range(3):
            x_copy(s).start()

    gather(3)
    x_copy(3).start()

    for copy in (*up, *dn, own, *sh_up, *sh_dn, *f1, *sh_f1):
        copy.wait_send()

    @pl.when(core == 0)
    def _():
        for copy in (*fd, *l_copies):
            copy.wait_send()

    for s in range(4):

        def sent(k, carry, s=s):
            z_copy(s, k).wait_send()
            return carry

        lax.fori_loop(1, N_Z, sent, 0)
    for s in range(3):
        finish(s, parts[s])
    finish(3, late)
    for s in range(4):
        x_copy(s).wait_send()

    @pl.when(core == 1)
    def _():
        o_ref[first_k[3, 0], :, :] = (tot[3] + xrecv[3])[0:take, pairs : 2 * pairs]

    @pl.when(core == 0)
    def _():
        final = all_sum(lsend, lrecv, l_copies)
        o_ref[first_k[3, 0], 0:top, :] = final[0:top, 0:pairs]
        o_ref[first_k[3, 0], top:take, :] = final[0 : take - top, pairs : 2 * pairs]


def shards(integrals, doubles, singles):
    rows, cols = integrals.shape
    pairs = doubles.shape[0]
    occ, virt = singles.shape
    n_ab, n_cd = lax.axis_size("ab"), lax.axis_size("cd")
    steps = n_ab // 4
    take = rows // n_cd
    dma = pltpu.SemaphoreType.DMA
    return pl.pallas_call(
        kernel,
        out_shape=jax.ShapeDtypeStruct((steps, take, pairs), F32),
        in_specs=[pl.BlockSpec(memory_space=pl.ANY)] * 3,
        out_specs=pl.BlockSpec(memory_space=pltpu.VMEM),
        scratch_shapes=[
            pltpu.VMEM((rows, cols), BF16),
            pltpu.VMEM((occ, virt), F32),
            pltpu.VMEM((4, 2, pairs, cols), BF16),
            pltpu.VMEM((occ + 32, cols), F32),
            pltpu.VMEM((16, 8, cols), F32),
            pltpu.VMEM((rows + 8, 2 * pairs), F32),
            pltpu.VMEM((rows + 8, pairs), F32),
            pltpu.VMEM((4, N_Z, n_cd // N_Z, 32, 2 * pairs), BF16),
            pltpu.VMEM((4, N_Z - 1, n_cd // N_Z, 32, 2 * pairs), BF16),
            pltpu.VMEM((4, 32, 2 * pairs), F32),
            pltpu.VMEM((4, 32, 2 * pairs), F32),
            pltpu.VMEM((4, 32, 2 * pairs), F32),
            pltpu.VMEM((n_cd, 16, 2 * pairs), BF16),
            pltpu.VMEM((n_cd - 1, 16, 2 * pairs), BF16),
            dma((3,)),
            dma((3,)), dma((3,)), dma((2,)), dma((2,)), dma((2,)), dma((2,)),
            dma((2,)), dma((2,)), dma((len(CUTS),)), dma((2, len(CUTS))),
            dma((7,)), dma((7,)),
            dma((4, N_Z - 1)), dma((4, N_Z - 1)),
            dma((4,)), dma((4,)),
            dma((n_cd - 1,)), dma((n_cd - 1,)),
        ],
        compiler_params=pltpu.CompilerParams(
            collective_id=0, has_side_effects=True, vmem_limit_bytes=VMEM_GRANT
        ),
        cost_estimate=pl.CostEstimate(
            flops=2 * rows * cols * steps * pairs, bytes_accessed=2 * (rows + pairs) * cols, transcendentals=0
        ),
    )(integrals, doubles, singles)


def solution(mesh):
    in_specs = (P("ab", "cd"), P("ab", "cd"), P())
    out_specs = P(None, ("ab", "cd"), None)
    return jax.shard_map(shards, mesh=mesh, in_specs=in_specs, out_specs=out_specs, check_vma=False)
```

```python
import functools

import jax
import jax.numpy as jnp
from jax import lax
from jax.experimental import pallas as pl
from jax.experimental.pallas import tpu as pltpu
from jax.sharding import PartitionSpec as P

MESH = pl.DeviceIdType.MESH
F32 = jnp.float32
BF16 = jnp.bfloat16
N_Z = 8
KC = 2048
VMEM_GRANT = 53 * 2**20 + 704 * 2**10
CUTS = (0, 2048, 4096)


def kernel(
    a_hbm, d_hbm, s_hbm, o_ref,
    a_v, s_v, slots, rtab, ltab, acc, acc_l,
    sbuf, rbuf, xsend, xrecv, tot, lsend, lrecv,
    loc_sem, up_s, up_r, dn_s, dn_r, fd_s, fd_r, f1_s, f1_r, f0_s, f0_r, sib_s, sib_r,
    z_s, z_r, x_s, x_r, l_s, l_r,
):
    pairs, cols = d_hbm.shape
    rows = a_hbm.shape[0]
    occ, virt = s_hbm.shape
    c_local = cols // virt
    n_ab = lax.axis_size("ab")
    n_cd = lax.axis_size("cd")
    n_x = n_cd // N_Z
    take = rows // n_cd
    half = pairs // 2

    ab = lax.axis_index("ab")
    cd = lax.axis_index("cd")
    core = lax.rem(ab, 2)
    chip2 = ab - core
    x_hi = cd // N_Z
    z = lax.rem(cd, N_Z)

    nxt = {"ab": lax.rem(ab + 2, n_ab)}
    prv = {"ab": lax.rem(ab + n_ab - 2, n_ab)}
    sib = {"ab": ab + 1 - 2 * core}
    low = {"ab": lax.rem(ab + n_ab - 1, n_ab)}
    high = {"ab": lax.rem(ab + 1, n_ab)}
    nxt0 = {"ab": lax.rem(chip2 + 2, n_ab)}

    bar = pltpu.get_barrier_semaphore()
    for peer in (nxt, prv, low, high):
        pl.semaphore_signal(bar, inc=1, device_id=peer, device_id_type=MESH)

    for k in (0, 1, 7, 2, 6, 3, 5, 4):
        for x in (1, 0):
            if x or k:
                member = {"cd": lax.rem(x_hi + x, n_x) * N_Z + lax.rem(z + k, N_Z)}
                pl.semaphore_signal(bar, inc=1, device_id=member, device_id_type=MESH)


    load_s = pltpu.make_async_copy(s_hbm, s_v, loc_sem.at[0])
    load_d = pltpu.make_async_copy(d_hbm, slots.at[0, core], loc_sem.at[1])
    load_a = pltpu.make_async_copy(a_hbm, a_v, loc_sem.at[2])
    load_d.start()
    load_s.start()
    load_a.start()

    pl.semaphore_wait(bar, n_cd + 3)

    def remote(src, dst, ss, rs, dev):
        return pltpu.make_async_remote_copy(
            src_ref=src, dst_ref=dst, send_sem=ss, recv_sem=rs, device_id=dev, device_id_type=MESH
        )

    part = [pl.ds(pl.multiple_of(half * r, 32), half) for r in (core, 1 - core)]
    other = [pl.ds(pl.multiple_of(half * r, 32), half) for r in (1 - core, core)]
    quarter = half // 2
    halved = [pl.ds(pl.multiple_of(half * (1 - core) + quarter * j, 16), quarter) for j in range(2)]
    up_rows = [part[0], *halved]
    up = [remote(slots.at[0, core, q], slots.at[1, core, q], up_s.at[i], up_r.at[i], nxt) for i, q in enumerate(up_rows)]
    dn = [remote(slots.at[0, core, q], slots.at[2, core, q], dn_s.at[i], dn_r.at[i], prv) for i, q in enumerate(part)]
    own = remote(slots.at[0, core], slots.at[0, core], sib_s.at[5], sib_r.at[5], sib)
    sh_up = [remote(slots.at[1, core, q], slots.at[1, core, q], sib_s.at[i], sib_r.at[i], sib) for i, q in enumerate(part)]
    sh_dn = [remote(slots.at[2, core, q], slots.at[2, core, q], sib_s.at[2 + i], sib_r.at[2 + i], sib) for i, q in enumerate(part)]
    f1 = [remote(slots.at[1, 1, q], slots.at[3, 1, q], f1_s.at[j], f1_r.at[j], nxt) for j, q in enumerate(halved)]
    sh_f1 = [remote(slots.at[3, 1, q], slots.at[3, 1, q], sib_s.at[j], sib_r.at[j], sib) for j, q in zip((4, 6), halved)]
    ends = (*CUTS[1:], cols)
    spans = [pl.ds(a, b - a) for a, b in zip(CUTS, ends)]
    f0 = [
        remote(slots.at[1, 0, part[0], c], slots.at[3, 0, part[0], c], f0_s.at[j], f0_r.at[core, j], nxt0)
        for j, c in enumerate(spans)
    ]
    f0_in = [
        [
            remote(slots.at[1, 0, q, c], slots.at[3, 0, q, c], f0_s.at[j], f0_r.at[i, j], nxt0)
            for i, q in enumerate((pl.ds(0, half), pl.ds(half, half)))
        ]
        for j, c in enumerate(spans)
    ]
    fd = [remote(slots.at[2, core, q], slots.at[3, core, q], fd_s.at[i], fd_r.at[i], low) for i, q in enumerate(part)]
    fd_in = [remote(slots.at[2, 0, q], slots.at[3, 0, q], fd_s.at[i], fd_r.at[i], low) for i, q in enumerate(other)]

    load_d.wait()
    up[0].start()
    dn[0].start()
    own.start()
    up[1].start()
    up[2].start()
    dn[1].start()

    load_s.wait()

    def spread(t, carry):
        rows_t = s_v[pl.ds(pl.multiple_of(lax.rem(32 * t, occ), 32), 32), :]
        at = pl.ds(pl.multiple_of(32 * t, 32), 32)
        for c in range(c_local):
            rtab[at, c * virt : (c + 1) * virt] = rows_t
        return carry

    lax.fori_loop(0, rtab.shape[0] // 32, spread, 0)
    few = s_v[0 : ltab.shape[0], :]
    lane = lax.broadcasted_iota(jnp.int32, few.shape, 1)
    for c in range(c_local):
        value = jnp.sum(jnp.where(lane == cd * c_local + c, few, 0.0), axis=1, keepdims=True)
        for i in range(few.shape[0]):
            ltab[i, :, c * virt : (c + 1) * virt] = jnp.broadcast_to(value[i : i + 1, :], (8, virt))

    far = jnp.where(core == 0, -4, 4)
    place = {(0, 0): 0, (0, 1): 1, (1, 0): -2, (1, 1): -1, (2, 0): 2, (2, 1): 3, (3, 0): far, (3, 1): -3}
    row = lax.rem(ab // 2, n_ab // 4)
    inner = jnp.logical_and(row > 0, row < n_ab // 4 - 1)
    first_k = {
        (0, 0): 3 + core, (0, 1): 2 + core, (1, 0): 5 + core, (1, 1): 4 + core,
        (2, 0): 1 + core, (2, 1): core, (3, 0): 7 - 7 * core, (3, 1): 6 + core,
    }

    def tau(slot, h, r0, count, ks, width):
        first = lax.rem(chip2 + place[slot, h] + n_ab, n_ab) * pairs
        i0 = first // occ
        turn = occ * (i0 + 1) - first
        raw = slots[slot, h, r0 : r0 + count, ks].astype(F32)
        right = rtab[pl.ds(pl.multiple_of(lax.rem(first, occ) + r0, 32), count), ks]
        pair = lax.broadcasted_iota(jnp.int32, (count, width), 0) + r0
        before, after = (jnp.concatenate([ltab[i, :, ks]] * (count // 8), axis=0) for i in (i0, i0 + 1))
        left = jnp.where(pair < turn, before, after)
        return (raw + left * right).astype(BF16)

    def product(parts, out, start=0, stop=None):
        total = sum(p[3] for p in parts)

        def piece(ks, width):
            formed = [tau(*p, ks, width) for p in parts]
            both = jnp.concatenate(formed, axis=0) if len(formed) > 1 else formed[0]
            return lax.dot_general(a_v[:, ks], both, (((1,), (1,)), ((), ())), preferred_element_type=F32)

        def step(t, carry):
            out[0:rows, 0:total] += piece(pl.ds(pl.multiple_of(t * KC, KC), KC), KC)
            return carry

        whole = cols // KC
        if stop is None:
            tail = piece(pl.ds(whole * KC, cols - whole * KC), cols - whole * KC)
            if start:
                out[0:rows, 0:total] += tail
            else:
                out[0:rows, 0:total] = tail
            lax.fori_loop(start, whole, step, 0)
        else:
            if start == 0:
                out[0:rows, 0:total] = piece(pl.ds(0, KC), KC)
            lax.fori_loop(max(start, 1), stop, step, 0)

    def put(value, parts):
        lane0 = 0
        for slot, h, r0, count in parts:
            o_ref[first_k[slot, h], :, r0 : r0 + count] = value[0:take, lane0 : lane0 + count]
            lane0 += count

    def z_copy(s, k):
        to = lax.rem(z + k, N_Z)
        return remote(
            sbuf.at[s, to], rbuf.at[s, k - 1], z_s.at[s, k - 1], z_r.at[s, k - 1], {"cd": x_hi * N_Z + to}
        )

    def scatter(s):
        for j in range(n_cd):
            sbuf[s, j % N_Z, j // N_Z, :, :] = acc[j * take : j * take + 32, :].astype(sbuf.dtype)

        for k in (4, 3, 5, 2, 6, 1, 7):
            z_copy(s, k).start()

    def x_copy(s):
        return remote(xsend.at[s], xrecv.at[s], x_s.at[s], x_r.at[s], {"cd": (1 - x_hi) * N_Z + z})

    def gather(s):
        def arrive(k, carry):
            z_copy(s, k).wait_recv()
            return carry

        lax.fori_loop(1, N_Z, arrive, 0)
        for dst, xo in ((xsend, 1 - x_hi), (tot, x_hi)):
            total = sbuf[s, z, xo].astype(F32)
            for k in range(N_Z - 1):
                total = total + rbuf[s, k, xo].astype(F32)
            dst[s] = total

        @pl.when(jnp.logical_and(inner, s < 3))
        def _():
            x_copy(s).start()

    def finish(s, parts):
        x_copy(s).wait_recv()
        put(tot[s] + xrecv[s], parts)

    order = [(x, k) for k in (4, 3, 5, 2, 6, 1, 7, 0) for x in (1, 0) if x or k]

    def all_copies(send, recv, ss, rs):
        copies = []
        for x, k in order:
            to = lax.rem(x_hi + x, n_x) * N_Z + lax.rem(z + k, N_Z)
            n = 2 * k + x - 1
            copies.append(remote(send.at[to], recv.at[n], ss.at[n], rs.at[n], {"cd": to}))
        return copies

    def all_sum(send, recv, copies):
        for copy in reversed(copies):
            copy.wait_recv()
        value = send[cd].astype(F32)
        for n in range(n_cd - 1):
            value = value + recv[n].astype(F32)
        return value

    acc[rows:, :] = jnp.zeros((acc.shape[0] - rows, acc.shape[1]), F32)
    acc_l[rows:, :] = jnp.zeros((acc_l.shape[0] - rows, acc_l.shape[1]), F32)

    parts = [
        [(0, 0, 0, pairs), (0, 1, 0, pairs)],
        [(1, 0, 0, half), (1, 1, half, half), (2, 0, 0, half), (2, 1, half, half)],
        [(1, 0, half, half), (1, 1, 0, half), (2, 0, half, half), (2, 1, 0, half)],
    ]
    late = [(3, 1, 0, pairs)]
    late_1 = [(3, 1, 0, pairs), (3, 0, 0, pairs)]
    last = [(3, 0, 0, pairs)]
    top = (take + 1) // 2

    load_a.wait()
    own.wait_recv()
    product(parts[0], acc)
    scatter(0)

    sh_up_in = [remote(slots.at[1, 1 - core, q], slots.at[1, 1 - core, q], sib_s.at[i], sib_r.at[i], sib) for i, q in enumerate(other)]
    sh_dn_in = [remote(slots.at[2, 1 - core, q], slots.at[2, 1 - core, q], sib_s.at[2 + i], sib_r.at[2 + i], sib) for i, q in enumerate(other)]
    theirs = [pl.ds(pl.multiple_of(half * core + quarter * j, 16), quarter) for j in range(2)]
    sh_f1_in = [remote(slots.at[3, 1, q], slots.at[3, 1, q], sib_s.at[j], sib_r.at[j], sib) for j, q in zip((4, 6), theirs)]

    up[0].wait_recv()
    sh_up[0].start()
    dn[0].wait_recv()
    sh_dn[0].start()

    @pl.when(core == 0)
    def _():
        fd[0].start()

    sh_up_in[0].wait_recv()

    @pl.when(core == 0)
    def _():
        f1[0].start()
        f1[1].start()
        for copy in f0:
            copy.start()

    sh_dn_in[0].wait_recv()
    product(parts[1], acc)
    scatter(1)

    up[1].wait_recv()

    @pl.when(core == 1)
    def _():
        f1[0].start()

    up[2].wait_recv()
    sh_up[1].start()

    @pl.when(core == 1)
    def _():
        f1[1].start()

    dn[1].wait_recv()
    sh_dn[1].start()

    @pl.when(core == 0)
    def _():
        fd[1].start()

    sh_up_in[1].wait_recv()

    @pl.when(core == 1)
    def _():
        for copy in f0:
            copy.start()

    sh_dn_in[1].wait_recv()
    product(parts[2], acc)
    scatter(2)
    gather(0)
    gather(1)

    for j in range(2):
        f1[j].wait_recv()
        sh_f1[j].start()
    l_copies = all_copies(lsend, lrecv, l_s, l_r)

    @pl.when(core == 0)
    def _():
        for copy in sh_f1_in:
            copy.wait_recv()
        product(late, acc)

    @pl.when(core == 1)
    def _():
        fd_in[0].wait_recv()
        fd_in[1].wait_recv()
        for copy in sh_f1_in:
            copy.wait_recv()
        product(late_1, acc)

    scatter(3)
    gather(2)

    @pl.when(core == 0)
    def _():
        for j, copies in enumerate(f0_in):
            for copy in copies:
                copy.wait_recv()
            product(last, acc_l, CUTS[j] // KC, ends[j] // KC if j + 1 < len(CUTS) else None)
        for j in range(n_cd):
            halves = [acc_l[j * take + r : j * take + r + 16, :] for r in (0, top)]
            lsend[j, :, :] = jnp.concatenate(halves, axis=1).astype(lsend.dtype)
        def send(t, carry):
            x = n_x - 1 - lax.rem(t, n_x)
            k = lax.rem(t // n_x - z + N_Z, N_Z)

            @pl.when(x + k > 0)
            def _():
                to = lax.rem(x_hi + x, n_x) * N_Z + t // n_x
                n = n_x * k + x - 1
                remote(lsend.at[to], lrecv.at[n], l_s.at[n], l_r.at[n], {"cd": to}).start()

            return carry

        lax.fori_loop(0, n_cd, send, 0)

    for copy in f0:
        copy.wait_send()

    @pl.when(jnp.logical_not(inner))
    def _():
        for s in range(3):
            x_copy(s).start()

    gather(3)
    x_copy(3).start()

    for copy in (*up, *dn, own, *sh_up, *sh_dn, *f1, *sh_f1):
        copy.wait_send()

    @pl.when(core == 0)
    def _():
        for copy in (*fd, *l_copies):
            copy.wait_send()

    for s in range(4):

        def sent(k, carry, s=s):
            z_copy(s, k).wait_send()
            return carry

        lax.fori_loop(1, N_Z, sent, 0)
    for s in range(3):
        finish(s, parts[s])
    finish(3, late)
    for s in range(4):
        x_copy(s).wait_send()

    @pl.when(core == 1)
    def _():
        o_ref[first_k[3, 0], :, :] = (tot[3] + xrecv[3])[0:take, pairs : 2 * pairs]

    @pl.when(core == 0)
    def _():
        final = all_sum(lsend, lrecv, l_copies)
        o_ref[first_k[3, 0], 0:top, :] = final[0:top, 0:pairs]
        o_ref[first_k[3, 0], top:take, :] = final[0 : take - top, pairs : 2 * pairs]


def shards(integrals, doubles, singles):
    rows, cols = integrals.shape
    pairs = doubles.shape[0]
    occ, virt = singles.shape
    n_ab, n_cd = lax.axis_size("ab"), lax.axis_size("cd")
    steps = n_ab // 4
    take = rows // n_cd
    dma = pltpu.SemaphoreType.DMA
    return pl.pallas_call(
        kernel,
        out_shape=jax.ShapeDtypeStruct((steps, take, pairs), F32),
        in_specs=[pl.BlockSpec(memory_space=pl.ANY)] * 3,
        out_specs=pl.BlockSpec(memory_space=pltpu.VMEM),
        scratch_shapes=[
            pltpu.VMEM((rows, cols), BF16),
            pltpu.VMEM((occ, virt), F32),
            pltpu.VMEM((4, 2, pairs, cols), BF16),
            pltpu.VMEM((occ + 32, cols), F32),
            pltpu.VMEM((16, 8, cols), F32),
            pltpu.VMEM((rows + 8, 2 * pairs), F32),
            pltpu.VMEM((rows + 8, pairs), F32),
            pltpu.VMEM((4, N_Z, n_cd // N_Z, 32, 2 * pairs), BF16),
            pltpu.VMEM((4, N_Z - 1, n_cd // N_Z, 32, 2 * pairs), BF16),
            pltpu.VMEM((4, 32, 2 * pairs), F32),
            pltpu.VMEM((4, 32, 2 * pairs), F32),
            pltpu.VMEM((4, 32, 2 * pairs), F32),
            pltpu.VMEM((n_cd, 16, 2 * pairs), BF16),
            pltpu.VMEM((n_cd - 1, 16, 2 * pairs), BF16),
            dma((3,)),
            dma((3,)), dma((3,)), dma((2,)), dma((2,)), dma((2,)), dma((2,)),
            dma((2,)), dma((2,)), dma((len(CUTS),)), dma((2, len(CUTS))),
            dma((7,)), dma((7,)),
            dma((4, N_Z - 1)), dma((4, N_Z - 1)),
            dma((4,)), dma((4,)),
            dma((n_cd - 1,)), dma((n_cd - 1,)),
        ],
        compiler_params=pltpu.CompilerParams(
            collective_id=0, has_side_effects=True, vmem_limit_bytes=VMEM_GRANT
        ),
        cost_estimate=pl.CostEstimate(
            flops=2 * rows * cols * steps * pairs, bytes_accessed=2 * (rows + pairs) * cols, transcendentals=0
        ),
    )(integrals, doubles, singles)


def solution(mesh):
    in_specs = (P("ab", "cd"), P("ab", "cd"), P())
    out_specs = P(None, ("ab", "cd"), None)
    return jax.shard_map(shards, mesh=mesh, in_specs=in_specs, out_specs=out_specs, check_vma=False)
```
